32 devices in a mesh: rows: 8 (over z, x), feat: 4 (over y, core).
Axes of the slice: x: 2, y: 2, z: 4, core: 2. Of those that a mesh axis runs over, the one named last changes fastest.
Arguments:
- binned: int32 [16384, 256], P('rows', 'feat'), may hold values from 0 to 255
- node_index: int32 [16384, 1], P('rows'), may hold values from 0 to 7; in each aligned block of 2048 rows (0 to 2047, 2048 to 4095, ...) at most 512 rows name the same one
- treatment: float32 [16384], P('rows'), may hold values from -6 to 6
- outcome: float32 [16384], P('rows'), may hold values from -6 to 6
- unit_weight: float32 [16384], P('rows'), may hold values from 0.1 to 2
- root_feature: int32 [8], replicated, may hold values from 0 to 255
- root_cutoff: int32 [8], replicated, may hold values from 64 to 191
- child_feature: int32 [16], replicated, may hold values from 0 to 255
- child_cutoff: int32 [16], replicated, may hold values from 64 to 191
Outputs:
- node_moments: float32 [8, 3, 256, 256], P('rows', None, 'feat')
- child_moments: float32 [16, 3, 256, 256], P('rows', None, 'feat')
- leaf_moments: float32 [32, 3, 256, 256], P('rows', None, 'feat')
The draws below stay inside these ranges and needn't reach their ends.
Inputs may be any that keep to these rules, and one draw needn't show every extreme that they name: `node_index`: among the rows of one device no node is named by more than 512 rows, a bound that some block reaches.
All inputs are finite; a program needn't handle non-finite values.
Results may differ from the reference program's by a relative error of at most 0.0022.
Values may be sent and summed in bfloat16 or wider, within the bound.
A program may use at most 64 MiB of HBM per device.

```python
import math
import jax
import jax.numpy as jnp
import numpy as np
from jax import lax

FEATURES = 256
BINS = 256
ROW_DEV = 2048
ROWS = 16384
NODES = 8
CAPACITY = 512


def touch_ends(entries, rng, least, top_value):
    dims = entries.shape
    spot = [jax.random.randint(jax.random.fold_in(rng, axis), (), 0, dims[axis]) for axis in range(len(dims))]
    entries = entries.at[tuple(spot)].set(least)
    longest = dims.index(max(dims))
    spot[longest] = (spot[longest] + 1) % dims[longest]
    return entries.at[tuple(spot)].set(top_value)


def levels(own_key, shape, cuts, least, top_value):
    factor_of, own = 1.0, jax.random.fold_in(own_key, 6)
    for position, parts in cuts:
        steps = jnp.exp(jax.random.uniform(jax.random.fold_in(own, position), (parts,), jnp.float32, least / len(cuts), top_value / len(cuts)))
        factor_of = factor_of * jnp.repeat(steps, shape[position] // parts).reshape([-1 if axis == position else 1 for axis in range(len(shape))])
    return factor_of


def shared_out(rng, own, number, rows, number_of, top, limit, slope):
    order = jax.random.permutation(rng, number_of)
    packed, common = shares(number_of, rows * top, limit, slope, True), shares(number_of, rows * top, limit, slope, False)
    places = jnp.arange(number_of)

    def named(sizes, offset_by):
        used = int((sizes > 0).sum())
        fixed = max(1, used // 4)
        shifted = fixed + (places - fixed + offset_by * (used - fixed)) % max(1, number_of - fixed)
        return jnp.zeros((number_of,), jnp.int32).at[order[jnp.where(places < fixed, places, shifted)]].set(jnp.asarray(sizes, jnp.int32))

    sizes = jnp.where(number % 4 == 0, named(packed, number // 4), named(common, number - number // 4 - 1))
    mixed = jax.random.permutation(jax.random.fold_in(own, 3), number_of)
    donor, taker = mixed[0:number_of // 2 * 2:2], mixed[1:number_of // 2 * 2:2]
    slack = jnp.minimum(sizes[donor] - 1, limit - sizes[taker]) // 2
    slack = jnp.where((donor == order[0]) | (taker == order[0]) | (sizes[taker] == 0), 0, jnp.maximum(slack, 0))
    shifted = jax.random.randint(jax.random.fold_in(own, 4), (number_of // 2,), 0, 1 << 20) % (slack + 1)
    sizes = sizes.at[donor].add(-shifted).at[taker].add(shifted)
    members = jnp.searchsorted(jnp.cumsum(sizes), jnp.arange(rows * top), side="right").astype(jnp.int32)
    listing = members.reshape(top, rows).T
    listing = listing[jax.random.permutation(jax.random.fold_in(own, 1), rows)]
    offset_by = jax.random.randint(jax.random.fold_in(own, 2), (rows, 1), 0, top)
    return jnp.take_along_axis(listing, (jnp.arange(top)[None, :] + offset_by) % top, axis=1)


def shares(count, total, most, lean, full):
    loads = [(1 << 20) // math.isqrt(grade ** lean) + 1 for grade in range(1, count + 1)]
    largest = most if full else min(most, max(-(-total // count), total * loads[0] // sum(loads)))
    least = 1 if total - largest >= count - 1 else 0
    holding, spare = [largest] + [least] * (count - 1), total - largest - least * (count - 1)
    while spare > 0:
        free = [i for i in range(1, count) if holding[i] < largest] or [i for i in range(1, count) if holding[i] < most]
        pool, budget = sum([loads[i] for i in free]), spare
        for i in free:
            addition = min(most - holding[i], max(1, budget * loads[i] // pool), spare)
            holding[i] = holding[i] + addition
            spare = spare - addition
    return np.array(holding)


def centred(stream_key, shape, spread, bound, pieces=(), kind=jnp.bfloat16):
    loudness = levels(stream_key, shape, pieces, -0.22, 0.18) if pieces else 1.0
    drawn = jax.random.normal(stream_key, shape, jnp.float32) * spread * loudness
    return jnp.minimum(jnp.maximum(drawn, -bound), bound).astype(kind)


def setup_inputs(seed: int = 0) -> dict:
    key_list = jax.random.split(jax.random.key(seed), 10)
    binned = touch_ends(jax.random.randint(key_list[0], (ROWS, FEATURES), 0, BINS), jax.random.fold_in(key_list[0], 1), 0, BINS - 1).astype(jnp.int32)
    node_index_keys = jax.random.split(jax.random.fold_in(key_list[1], 1), ROWS // ROW_DEV)
    node_index_turns = jax.random.permutation(jax.random.fold_in(key_list[1], 3), ROWS // ROW_DEV)
    node_index = jax.vmap(lambda own, number: shared_out(jax.random.fold_in(key_list[1], 2), own, number, ROW_DEV, NODES, 1, CAPACITY, 1))(node_index_keys, node_index_turns).reshape((ROWS, 1))
    treatment = centred(key_list[2], (ROWS,), 1.0, 6.0, ((0, 8),), jnp.float32)
    outcome = centred(key_list[3], (ROWS,), 1.0, 6.0, ((0, 8),), jnp.float32)
    unit_weight = jnp.clip(jnp.exp(math.log(2.0) - 2.9957323 * jax.random.uniform(key_list[4], (ROWS,), jnp.float32) ** levels(key_list[4], (ROWS,), ((0, 8),), -0.2, 0.2)), 0.1, 2.0)
    root_feature = touch_ends(jax.random.randint(key_list[5], (NODES,), 0, FEATURES), jax.random.fold_in(key_list[5], 1), 0, FEATURES - 1).astype(jnp.int32)
    root_cutoff = touch_ends(jax.random.randint(key_list[6], (NODES,), BINS // 4, 3 * BINS // 4), jax.random.fold_in(key_list[6], 1), BINS // 4, (3 * BINS // 4) - 1).astype(jnp.int32)
    child_feature = touch_ends(jax.random.randint(key_list[7], (2 * NODES,), 0, FEATURES), jax.random.fold_in(key_list[7], 1), 0, FEATURES - 1).astype(jnp.int32)
    child_cutoff = touch_ends(jax.random.randint(key_list[8], (2 * NODES,), BINS // 4, 3 * BINS // 4), jax.random.fold_in(key_list[8], 1), BINS // 4, (3 * BINS // 4) - 1).astype(jnp.int32)
    return {"binned": binned, "node_index": node_index, "treatment": treatment, "outcome": outcome, "unit_weight": unit_weight, "root_feature": root_feature, "root_cutoff": root_cutoff, "child_feature": child_feature, "child_cutoff": child_cutoff}


def reference(binned, node_index, treatment, outcome, unit_weight, root_feature, root_cutoff, child_feature, child_cutoff):
    tree_node = node_index[:, 0]
    rounded = jnp.stack([unit_weight, unit_weight * treatment * treatment, unit_weight * treatment * outcome], 1).astype(jnp.bfloat16)
    moments = lax.optimization_barrier(rounded).astype(jnp.float32)
    positions = jnp.arange(ROWS, dtype=jnp.int32)
    root_bins = binned[positions, root_feature[tree_node]]
    right_root = (root_bins > root_cutoff[tree_node]).astype(jnp.int32)
    child_index = (2 * tree_node + right_root).astype(jnp.int32)
    child_bins = binned[positions, child_feature[child_index]]
    right_child = (child_bins > child_cutoff[child_index]).astype(jnp.int32)
    leaf_index = (2 * child_index + right_child).astype(jnp.int32)

    def per_feature(column):
        segment_ids = (leaf_index * BINS + column).astype(jnp.int32)
        return jax.ops.segment_sum(moments, segment_ids, num_segments=4 * NODES * BINS)

    totals = lax.map(per_feature, binned.T)
    leaf_moments = totals.reshape(FEATURES, 4 * NODES, BINS, 3).transpose(1, 3, 0, 2)
    child_moments = leaf_moments.reshape(2 * NODES, 2, 3, FEATURES, BINS).sum(1)
    node_moments = leaf_moments.reshape(NODES, 4, 3, FEATURES, BINS).sum(1)
    return node_moments, child_moments, leaf_moments
```

```python
import functools

import jax
import jax.numpy as jnp
from jax import lax
from jax.experimental import pallas as pl
from jax.experimental.pallas import tpu as pltpu
from jax.sharding import PartitionSpec as P

BINS = 256
MESH = pl.DeviceIdType.MESH
NT = (((1,), (1,)), ((), ()))
EXTRA = 16


def exchange_kernel(
    owners,
    feat_devs,
    node_count,
    capacity,
    bins_ref,
    node_ref,
    units_ref,
    pick_ref,
    cut_ref,
    got_ref,
    pick_send,
    pick_recv,
    blocks,
    rows_in,
    slot_ref,
    pick_send_sem,
    pick_recv_sem,
    send_sem,
    recv_sem,
    self_sem,
):
    feat_here, rows_here = bins_ref.shape
    me = lax.axis_index("rows")
    mine = lax.axis_index("feat")

    barrier = pltpu.get_barrier_semaphore()
    for step in range(1, owners):
        pl.semaphore_signal(
            barrier, inc=1, device_id={"rows": lax.rem(me + step, owners)}, device_id_type=MESH
        )
    for step in range(1, feat_devs):
        pl.semaphore_signal(
            barrier, inc=1, device_id={"feat": lax.rem(mine + step, feat_devs)}, device_id_type=MESH
        )

    bins = bins_ref[...]
    node = node_ref[...]
    chosen = lax.broadcasted_iota(jnp.int32, (node_count, rows_here), 0) == node
    table = jnp.dot(pick_ref[...], bins, preferred_element_type=jnp.float32)
    picks, cuts = [], []
    for kind in range(3):
        part = table[kind * node_count : (kind + 1) * node_count]
        picks.append(jnp.sum(jnp.where(chosen, part, 0.0), axis=0, keepdims=True))
        limit = jnp.broadcast_to(cut_ref[:, kind : kind + 1], (node_count, rows_here))
        cuts.append(jnp.sum(jnp.where(chosen, limit, 0.0), axis=0, keepdims=True))
    picks.append(jnp.zeros_like(picks[0]))
    picks = jnp.concatenate(picks, axis=0)
    quarter = rows_here // 4
    folded = jnp.concatenate([picks[:, k * quarter : (k + 1) * quarter] for k in range(4)], axis=0)
    pick_send[...] = folded.astype(jnp.bfloat16)

    pl.semaphore_wait(barrier, owners - 1 + feat_devs - 1)

    pick_copies = []
    for step in range(1, feat_devs):
        copy = pltpu.make_async_remote_copy(
            src_ref=pick_send,
            dst_ref=pick_recv.at[step - 1],
            send_sem=pick_send_sem.at[step - 1],
            recv_sem=pick_recv_sem.at[step - 1],
            device_id={"feat": lax.rem(mine + step, feat_devs)},
            device_id_type=MESH,
        )
        copy.start()
        pick_copies.append(copy)

    chunk = 256
    ones = chosen.astype(jnp.float32)
    up_to = (
        lax.broadcasted_iota(jnp.int32, (chunk, chunk), 0)
        <= lax.broadcasted_iota(jnp.int32, (chunk, chunk), 1)
    ).astype(jnp.float32).astype(jnp.bfloat16)
    before = jnp.zeros((node_count, 1), jnp.float32)
    ranks = []
    for k in range(rows_here // chunk):
        here = ones[:, k * chunk : (k + 1) * chunk]
        counts = jnp.dot(here.astype(jnp.bfloat16), up_to, preferred_element_type=jnp.float32)
        counts = counts + before
        ranks.append(jnp.sum(here * counts, axis=0, keepdims=True))
        before = before + jnp.sum(here, axis=1, keepdims=True)
    rank = jnp.concatenate(ranks, axis=1).astype(jnp.int32) - 1
    slot_ref[...] = node * capacity + rank

    weight, treat, result = units_ref[0:1], units_ref[1:2], units_ref[2:3]
    scaled = weight * treat

    for copy in pick_copies:
        copy.wait()
    total = folded
    for step in range(feat_devs - 1):
        total = total + pick_recv[step].astype(jnp.float32)
    split = jnp.concatenate([total[4 * k : 4 * k + 4] for k in range(4)], axis=1)
    right_root = split[0:1] > cuts[0]
    first = jnp.where(split[1:2] > cuts[1], 1.0, 0.0)
    second = jnp.where(split[2:3] > cuts[2], 1.0, 0.0)
    leaf = jnp.where(right_root, 2.0 + second, first)
    extra = jnp.concatenate(
        [weight, scaled * treat, scaled * result, leaf, jnp.zeros((EXTRA - 4, rows_here), jnp.float32)],
        axis=0,
    ).astype(jnp.bfloat16)
    rows_in[0:feat_here] = bins
    rows_in[feat_here : feat_here + EXTRA] = extra

    place = lax.broadcasted_iota(jnp.int32, (capacity, rows_here), 0)

    def pack(owner):
        target = slot_ref[...] - owner * capacity
        here = jnp.where(place == target, 1.0, 0.0).astype(jnp.bfloat16)
        got = lax.dot_general(rows_in[...], here, NT, preferred_element_type=jnp.float32)
        blocks[owner] = got.astype(jnp.bfloat16)

    def send(step):
        owner = lax.rem(me + step, owners)
        return pltpu.make_async_remote_copy(
            src_ref=blocks.at[owner],
            dst_ref=got_ref.at[me],
            send_sem=send_sem.at[step - 1],
            recv_sem=recv_sem.at[step - 1],
            device_id={"rows": owner},
            device_id_type=MESH,
        )

    @pl.loop(1, owners)
    def _(step):
        pack(lax.rem(me + step, owners))
        send(step).start()

    pack(me)
    own = pltpu.make_async_copy(blocks.at[me], got_ref.at[me], self_sem)
    own.start()
    own.wait()

    @pl.loop(1, owners)
    def _(step):
        send(step).wait()


def histogram_kernel(got_ref, extra_ref, node_out, child_out, leaf_out):
    sources, group, capacity = got_ref.shape
    slots = sources * capacity
    bf = jnp.bfloat16
    extra = jnp.concatenate([extra_ref[s] for s in range(sources)], axis=1).astype(jnp.float32)
    row = lax.broadcasted_iota(jnp.int32, (16, slots), 0)
    kind = row % 3
    value = jnp.where(kind == 0, extra[0:1], jnp.where(kind == 1, extra[1:2], extra[2:3]))
    weights = jnp.where((row // 3).astype(jnp.float32) == extra[3:4], value, 0.0).astype(bf)
    bins = jnp.concatenate([got_ref[s] for s in range(sources)], axis=1).astype(jnp.float32)
    high = jnp.floor(bins * (1.0 / 64.0))
    low = (bins - 64.0 * high).astype(bf)
    high = high.astype(bf)
    level = lax.broadcasted_iota(jnp.int32, (16, slots), 0).astype(jnp.float32).astype(bf)
    one, zero = jnp.ones((), bf), jnp.zeros((), bf)
    lane = lax.broadcasted_iota(jnp.int32, (16, 128), 1)
    for base in range(0, group, 4):
        left, right = [], []
        for f in range(base, base + 4):
            high_f = jnp.broadcast_to(high[f : f + 1], (16, slots))
            low_f = jnp.broadcast_to(low[f : f + 1], (16, slots))
            for c in range(4):
                left.append(jnp.where(high_f == jnp.asarray(c, bf), weights, zero))
                right.append(jnp.where(low_f == level + jnp.asarray(16 * c, bf), one, zero))
        left = jnp.concatenate(left, axis=0)
        right = jnp.concatenate(right, axis=0)
        sums = lax.dot_general(left, right, NT, preferred_element_type=jnp.float32)
        for i in range(4):
            tile = 128 * (i // 2)
            parts = []
            for c in range(4):
                block = sums[64 * i + 16 * c : 64 * i + 16 * c + 16, tile : tile + 128]
                if c % 2 != i % 2:
                    block = pltpu.roll(block, 64, 1)
                parts.append(block)
            for t in range(2):
                full = jnp.where(lane < 64, parts[2 * t], parts[2 * t + 1])
                for q in range(4):
                    for m in range(3):
                        leaf_out[q, m, base + i : base + i + 1, 128 * t : 128 * t + 128] = full[
                            3 * q + m : 3 * q + m + 1
                        ]
    for m in range(3):
        a = leaf_out[0, m] + leaf_out[1, m]
        b = leaf_out[2, m] + leaf_out[3, m]
        child_out[0, m] = a
        child_out[1, m] = b
        node_out[0, m] = a + b


def on_device(
    owners,
    feat_devs,
    binned,
    node_index,
    treatment,
    outcome,
    unit_weight,
    root_feature,
    root_cutoff,
    child_feature,
    child_cutoff,
):
    rows_here, feat_here = binned.shape
    node_count = root_feature.shape[0]
    assert node_count == owners
    capacity = 2 * rows_here // node_count
    bf = jnp.bfloat16
    bins = binned.T.astype(bf)
    units = jnp.stack([unit_weight, treatment, outcome], 0)
    wanted = jnp.concatenate([root_feature, child_feature[0::2], child_feature[1::2]])
    wanted = wanted - lax.axis_index("feat") * feat_here
    pick = (wanted[:, None] == jnp.arange(feat_here)).astype(bf)
    cut = jnp.stack([root_cutoff, child_cutoff[0::2], child_cutoff[1::2]], 1).astype(jnp.float32)
    height = feat_here + EXTRA
    vmem = pl.BlockSpec(memory_space=pltpu.VMEM)
    dma = pltpu.SemaphoreType.DMA
    got = pl.pallas_call(
        functools.partial(exchange_kernel, owners, feat_devs, node_count, capacity),
        out_shape=jax.ShapeDtypeStruct((owners, height, capacity), bf),
        in_specs=[vmem] * 5,
        out_specs=pl.BlockSpec(memory_space=pl.ANY),
        scratch_shapes=[
            pltpu.VMEM((16, rows_here // 4), bf),
            pltpu.VMEM((feat_devs - 1, 16, rows_here // 4), bf),
            pltpu.VMEM((owners, height, capacity), bf),
            pltpu.VMEM((height, rows_here), bf),
            pltpu.VMEM((1, rows_here), jnp.int32),
            dma((feat_devs - 1,)),
            dma((feat_devs - 1,)),
            dma((owners - 1,)),
            dma((owners - 1,)),
            dma,
        ],
        compiler_params=pltpu.CompilerParams(
            collective_id=0, has_side_effects=True, vmem_limit_bytes=48 * 1024 * 1024
        ),
        name="exchange",
    )(bins, node_index.reshape(1, rows_here), units, pick, cut)

    group = 16
    return pl.pallas_call(
        histogram_kernel,
        grid=(feat_here // group,),
        out_shape=tuple(
            jax.ShapeDtypeStruct((k, 3, feat_here, BINS), jnp.float32) for k in (1, 2, 4)
        ),
        in_specs=[
            pl.BlockSpec((owners, group, capacity), lambda i: (0, i, 0)),
            pl.BlockSpec((owners, EXTRA, capacity), lambda i: (0, feat_here // EXTRA, 0)),
        ],
        out_specs=tuple(pl.BlockSpec((k, 3, group, BINS), lambda i: (0, 0, i, 0)) for k in (1, 2, 4)),
        compiler_params=pltpu.CompilerParams(vmem_limit_bytes=48 * 1024 * 1024),
        name="histogram",
    )(got, got)


def solution(mesh):
    in_specs = (
        P("rows", "feat"),
        P("rows", None),
        P("rows"),
        P("rows"),
        P("rows"),
        P(),
        P(),
        P(),
        P(),
    )
    out_specs = (P("rows", None, "feat", None),) * 3
    body = functools.partial(on_device, mesh.shape["rows"], mesh.shape["feat"])
    return jax.shard_map(body, mesh=mesh, in_specs=in_specs, out_specs=out_specs, check_vma=False)
```

```python
import functools

import jax
import jax.numpy as jnp
from jax import lax
from jax.experimental import pallas as pl
from jax.experimental.pallas import tpu as pltpu
from jax.sharding import PartitionSpec as P

BINS = 256
MESH = pl.DeviceIdType.MESH
NT = (((1,), (1,)), ((), ()))
EXTRA = 16
CHUNKS = 4
GROUP = 16
AHEAD = 4


def partner_of(me, step, owners):
    total, bit = 0, 1
    while bit < owners:
        total = total + lax.rem(me // bit + step // bit, 2) * bit
        bit *= 2
    return total


def weight_rows(extra):
    slots = extra.shape[1]
    row = lax.broadcasted_iota(jnp.int32, (16, slots), 0)
    kind = row % 3
    value = jnp.where(kind == 0, extra[0:1], jnp.where(kind == 1, extra[1:2], extra[2:3]))
    same = (row // 3).astype(jnp.float32) == extra[3:4]
    return jnp.where(same, value, 0.0).astype(jnp.bfloat16)


def pair_sums(bins, weights):
    slots = bins.shape[1]
    bf = jnp.bfloat16
    high = jnp.floor(bins * (1.0 / 64.0))
    low = (bins - 64.0 * high).astype(bf)
    high = high.astype(bf)
    level = lax.broadcasted_iota(jnp.int32, (16, slots), 0).astype(jnp.float32).astype(bf)
    one, zero = jnp.ones((), bf), jnp.zeros((), bf)
    lane = lax.broadcasted_iota(jnp.int32, (64, 128), 1)
    pairs = []
    for base in range(0, GROUP, 4):
        left, right = [], []
        for f in range(base, base + 4):
            high_f = jnp.broadcast_to(high[f : f + 1], (16, slots))
            low_f = jnp.broadcast_to(low[f : f + 1], (16, slots))
            for c in range(4):
                left.append(jnp.where(high_f == jnp.asarray(c, bf), weights, zero))
                right.append(jnp.where(low_f == level + jnp.asarray(16 * c, bf), one, zero))
        left = jnp.concatenate(left, axis=0)
        right = jnp.concatenate(right, axis=0)
        sums = lax.dot_general(left, right, NT, preferred_element_type=jnp.float32)
        for i in range(2):
            even = sums[128 * i : 128 * i + 64, 128 * i : 128 * i + 128]
            odd = sums[128 * i + 64 : 128 * i + 128, 128 * i : 128 * i + 128]
            pairs.append(jnp.where(lane < 64, even, odd))
    return pairs


def exchange_kernel(
    owners,
    feat_devs,
    node_count,
    capacity,
    bins_hbm,
    node_hbm,
    weight_hbm,
    treat_hbm,
    result_hbm,
    root_feat_hbm,
    root_cut_hbm,
    child_feat_hbm,
    child_cut_hbm,
    late_ref,
    acc_ref,
    bins_in,
    node_in,
    weight_in,
    treat_in,
    result_in,
    root_feat_in,
    root_cut_in,
    child_feat_in,
    child_cut_in,
    pick_send,
    pick_recv,
    blocks,
    got,
    rows_in,
    slot_ref,
    places,
    weights_ref,
    in_sem,
    pick_send_sem,
    pick_recv_sem,
    send_sem,
    recv_sem,
):
    feat_here, rows_here = bins_in.shape
    me = lax.axis_index("rows")
    mine = lax.axis_index("feat")
    bf = jnp.bfloat16

    pairs = [
        (node_hbm, node_in),
        (bins_hbm, bins_in),
        (root_feat_hbm, root_feat_in),
        (child_feat_hbm, child_feat_in),
        (root_cut_hbm, root_cut_in),
        (child_cut_hbm, child_cut_in),
        (weight_hbm, weight_in),
        (treat_hbm, treat_in),
        (result_hbm, result_in),
    ]
    loads = [pltpu.make_async_copy(a, b, in_sem.at[k]) for k, (a, b) in enumerate(pairs)]
    for load in loads:
        load.start()

    barrier = pltpu.get_barrier_semaphore()
    for step in range(1, owners):
        pl.semaphore_signal(
            barrier,
            inc=1,
            device_id={"rows": partner_of(me, step, owners)},
            device_id_type=MESH,
        )
    for step in range(1, feat_devs):
        pl.semaphore_signal(
            barrier, inc=1, device_id={"feat": lax.rem(mine + step, feat_devs)}, device_id_type=MESH
        )

    for load in loads:
        load.wait()
    node = node_in[...]
    bins = bins_in[...].astype(jnp.float32).astype(bf)
    rows_in[0:feat_here] = bins
    chosen = lax.broadcasted_iota(jnp.int32, (node_count, rows_here), 0) == node

    def column(table, stride, first):
        width = table.shape[1]
        spot = lax.broadcasted_iota(jnp.int32, (node_count, width), 0) * stride + first
        lane = lax.broadcasted_iota(jnp.int32, (node_count, width), 1)
        picked = jnp.where(lane == spot, table.astype(jnp.float32), 0.0)
        return jnp.sum(picked, axis=1, keepdims=True)

    wanted = [
        column(root_feat_in[...], 1, 0),
        column(child_feat_in[...], 2, 0),
        column(child_feat_in[...], 2, 1),
    ]
    limits = [
        column(root_cut_in[...], 1, 0),
        column(child_cut_in[...], 2, 0),
        column(child_cut_in[...], 2, 1),
    ]
    local = lax.broadcasted_iota(jnp.int32, (node_count, feat_here), 1) + mine * feat_here
    local = local.astype(jnp.float32)
    pick = jnp.concatenate([jnp.where(local == w, 1.0, 0.0) for w in wanted], axis=0).astype(bf)
    table = jnp.dot(pick, bins, preferred_element_type=jnp.float32)
    picks, cuts = [], []
    for kind in range(3):
        part = table[kind * node_count : (kind + 1) * node_count]
        picks.append(jnp.sum(jnp.where(chosen, part, 0.0), axis=0, keepdims=True))
        limit = jnp.broadcast_to(limits[kind], (node_count, rows_here))
        cuts.append(jnp.sum(jnp.where(chosen, limit, 0.0), axis=0, keepdims=True))
    picks.append(jnp.zeros_like(picks[0]))
    picks = jnp.concatenate(picks, axis=0)
    quarter = rows_here // 4
    folded = jnp.concatenate([picks[:, k * quarter : (k + 1) * quarter] for k in range(4)], axis=0)
    pick_send[...] = folded.astype(bf)

    pl.semaphore_wait(barrier, owners - 1 + feat_devs - 1)

    pick_copies = []
    for step in range(1, feat_devs):
        copy = pltpu.make_async_remote_copy(
            src_ref=pick_send,
            dst_ref=pick_recv.at[step - 1],
            send_sem=pick_send_sem.at[step - 1],
            recv_sem=pick_recv_sem.at[step - 1],
            device_id={"feat": lax.rem(mine + step, feat_devs)},
            device_id_type=MESH,
        )
        copy.start()
        pick_copies.append(copy)

    chunk = 256
    ones = chosen.astype(jnp.float32)
    up_to = lax.broadcasted_iota(jnp.int32, (chunk, chunk), 0) <= lax.broadcasted_iota(
        jnp.int32, (chunk, chunk), 1
    )
    up_to = up_to.astype(jnp.float32).astype(bf)
    before = jnp.zeros((node_count, 1), jnp.float32)
    ranks = []
    for k in range(rows_here // chunk):
        here = ones[:, k * chunk : (k + 1) * chunk]
        counts = jnp.dot(here.astype(bf), up_to, preferred_element_type=jnp.float32) + before
        ranks.append(jnp.sum(here * counts, axis=0, keepdims=True))
        before = before + jnp.sum(here, axis=1, keepdims=True)
    rank = jnp.concatenate(ranks, axis=1).astype(jnp.int32) - 1
    slot_ref[...] = node * capacity + rank

    weight, treat, result = weight_in[...], treat_in[...], result_in[...]
    scaled = weight * treat
    place = lax.broadcasted_iota(jnp.int32, (capacity, rows_here), 0)

    def fill(step, where):
        target = slot_ref[...] - partner_of(me, step, owners) * capacity
        places[where] = jnp.where(place == target, 1.0, 0.0).astype(bf)

    half = owners // 2

    @pl.loop(0, AHEAD)
    def _(k):
        fill(half + k, k)

    for copy in pick_copies:
        copy.wait()
    total = folded
    for step in range(feat_devs - 1):
        total = total + pick_recv[step].astype(jnp.float32)
    split = jnp.concatenate([total[4 * k : 4 * k + 4] for k in range(4)], axis=1)
    right_root = split[0:1] > cuts[0]
    first = jnp.where(split[1:2] > cuts[1], 1.0, 0.0)
    second = jnp.where(split[2:3] > cuts[2], 1.0, 0.0)
    leaf = jnp.where(right_root, 2.0 + second, first)
    none = jnp.zeros((EXTRA - 4, rows_here), jnp.float32)
    extra = jnp.concatenate([weight, scaled * treat, scaled * result, leaf, none], axis=0)
    rows_in[feat_here : feat_here + EXTRA] = extra.astype(bf)

    def packed(where):
        moved = lax.dot_general(rows_in[...], places[where], NT, preferred_element_type=jnp.float32)
        return moved.astype(bf)

    per = owners // CHUNKS
    late_first = owners - per

    def send(step, late):
        place_there = late_ref.at[step - late_first] if late else got.at[step]
        return pltpu.make_async_remote_copy(
            src_ref=blocks.at[step],
            dst_ref=place_there,
            send_sem=send_sem.at[step],
            recv_sem=recv_sem.at[step],
            device_id={"rows": partner_of(me, step, owners)},
            device_id_type=MESH,
        )

    def each(start, stop, late, prepared):
        @pl.loop(start, stop)
        def _(step):
            where = lax.rem(step, AHEAD)
            if not prepared:
                fill(step, where)
            blocks[step] = packed(where)
            send(step, late).start()

    early = half + AHEAD
    for start, stop, prepared in ((half, early, True), (early, owners, False)):
        if start < min(stop, late_first):
            each(start, min(stop, late_first), False, prepared)
        if max(start, late_first) < stop:
            each(max(start, late_first), stop, True, prepared)
    while half > 1:
        half //= 2
        each(half, 2 * half, False, False)
    fill(0, 0)
    got[0] = packed(0)

    for c in range(CHUNKS - 1):
        for step in range(max(1, c * per), (c + 1) * per):
            send(step, False).wait_recv()
        known = got[c * per : (c + 1) * per, feat_here : feat_here + EXTRA]
        known = jnp.concatenate([known[s] for s in range(per)], axis=1).astype(jnp.float32)
        weights_ref[...] = weight_rows(known)

        @pl.loop(0, feat_here // GROUP)
        def _(block):
            rows = pl.ds(pl.multiple_of(block * GROUP, GROUP), GROUP)
            values = jnp.concatenate([got[c * per + s, rows] for s in range(per)], axis=1)
            sums = pair_sums(values.astype(jnp.float32), weights_ref[...])
            for k, part in enumerate(sums):
                spot = block * (GROUP // 2) + k
                acc_ref[spot] = part if c == 0 else acc_ref[spot] + part

    for step in range(1, owners):
        send(step, step >= late_first).wait_send()
    for step in range(late_first, owners):
        send(step, True).wait_recv()


def finish_kernel(late_ref, extra_ref, acc_ref, node_out, child_out, leaf_out):
    sources = late_ref.shape[0]
    extra = jnp.concatenate([extra_ref[s] for s in range(sources)], axis=1).astype(jnp.float32)
    bins = jnp.concatenate([late_ref[s] for s in range(sources)], axis=1).astype(jnp.float32)
    lane = lax.broadcasted_iota(jnp.int32, (16, 128), 1)
    for k, part in enumerate(pair_sums(bins, weight_rows(extra))):
        part = part + acc_ref[k]
        parts = [part[16 * c : 16 * c + 16] for c in range(4)]
        turned = [pltpu.roll(p, 64, 1) for p in parts]
        for i in range(2):
            f = 2 * k + i
            for t in range(2):
                if i == 0:
                    full = jnp.where(lane < 64, parts[2 * t], turned[2 * t + 1])
                else:
                    full = jnp.where(lane < 64, turned[2 * t], parts[2 * t + 1])
                for q in range(4):
                    for m in range(3):
                        leaf_out[q, m, f : f + 1, 128 * t : 128 * t + 128] = full[
                            3 * q + m : 3 * q + m + 1
                        ]
    for m in range(3):
        a = leaf_out[0, m] + leaf_out[1, m]
        b = leaf_out[2, m] + leaf_out[3, m]
        child_out[0, m] = a
        child_out[1, m] = b
        node_out[0, m] = a + b


def on_device(
    owners,
    feat_devs,
    binned,
    node_index,
    treatment,
    outcome,
    unit_weight,
    root_feature,
    root_cutoff,
    child_feature,
    child_cutoff,
):
    rows_here, feat_here = binned.shape
    node_count = root_feature.shape[0]
    assert node_count == owners and owners >= 2 * AHEAD and owners & (owners - 1) == 0
    capacity = 2 * rows_here // node_count
    bf, f32, i32 = jnp.bfloat16, jnp.float32, jnp.int32
    height = feat_here + EXTRA
    per = owners // CHUNKS
    dma = pltpu.SemaphoreType.DMA
    anywhere = pl.BlockSpec(memory_space=pltpu.HBM)
    vmem = pl.BlockSpec(memory_space=pltpu.VMEM)
    late, acc = pl.pallas_call(
        functools.partial(exchange_kernel, owners, feat_devs, node_count, capacity),
        out_shape=(
            jax.ShapeDtypeStruct((per, height, capacity), bf),
            jax.ShapeDtypeStruct((feat_here // 2, 64, 128), f32),
        ),
        in_specs=[anywhere] * 9,
        out_specs=(anywhere, vmem),
        scratch_shapes=[
            pltpu.VMEM((feat_here, rows_here), i32),
            pltpu.VMEM((1, rows_here), i32),
            pltpu.VMEM((1, rows_here), f32),
            pltpu.VMEM((1, rows_here), f32),
            pltpu.VMEM((1, rows_here), f32),
            pltpu.VMEM((1, node_count), i32),
            pltpu.VMEM((1, node_count), i32),
            pltpu.VMEM((1, 2 * node_count), i32),
            pltpu.VMEM((1, 2 * node_count), i32),
            pltpu.VMEM((16, rows_here // 4), bf),
            pltpu.VMEM((feat_devs - 1, 16, rows_here // 4), bf),
            pltpu.VMEM((owners, height, capacity), bf),
            pltpu.VMEM((owners - per, height, capacity), bf),
            pltpu.VMEM((height, rows_here), bf),
            pltpu.VMEM((1, rows_here), i32),
            pltpu.VMEM((AHEAD, capacity, rows_here), bf),
            pltpu.VMEM((16, per * capacity), bf),
            dma((9,)),
            dma((feat_devs - 1,)),
            dma((feat_devs - 1,)),
            dma((owners,)),
            dma((owners,)),
        ],
        compiler_params=pltpu.CompilerParams(
            collective_id=0, has_side_effects=True, vmem_limit_bytes=64 * 1024 * 1024
        ),
        name="exchange",
    )(
        binned.T,
        node_index.reshape(1, rows_here),
        unit_weight.reshape(1, rows_here),
        treatment.reshape(1, rows_here),
        outcome.reshape(1, rows_here),
        root_feature.reshape(1, node_count),
        root_cutoff.reshape(1, node_count),
        child_feature.reshape(1, 2 * node_count),
        child_cutoff.reshape(1, 2 * node_count),
    )

    return pl.pallas_call(
        finish_kernel,
        grid=(feat_here // GROUP,),
        out_shape=tuple(
            jax.ShapeDtypeStruct((k, 3, feat_here, BINS), f32) for k in (1, 2, 4)
        ),
        in_specs=[
            pl.BlockSpec((per, GROUP, capacity), lambda i: (0, i, 0)),
            pl.BlockSpec((per, EXTRA, capacity), lambda i: (0, feat_here // EXTRA, 0)),
            pl.BlockSpec((GROUP // 2, 64, 128), lambda i: (i, 0, 0)),
        ],
        out_specs=tuple(pl.BlockSpec((k, 3, GROUP, BINS), lambda i: (0, 0, i, 0)) for k in (1, 2, 4)),
        compiler_params=pltpu.CompilerParams(vmem_limit_bytes=64 * 1024 * 1024),
        name="finish",
    )(late, late, acc)


def solution(mesh):
    in_specs = (
        P("rows", "feat"),
        P("rows", None),
        P("rows"),
        P("rows"),
        P("rows"),
        P(),
        P(),
        P(),
        P(),
    )
    out_specs = (P("rows", None, "feat", None),) * 3
    body = functools.partial(on_device, mesh.shape["rows"], mesh.shape["feat"])
    return jax.shard_map(body, mesh=mesh, in_specs=in_specs, out_specs=out_specs, check_vma=False)
```

```python
import functools

import jax
import jax.numpy as jnp
from jax import lax
from jax.experimental import pallas as pl
from jax.experimental.pallas import tpu as pltpu
from jax.sharding import PartitionSpec as P

BINS = 256
MESH = pl.DeviceIdType.MESH
NT = (((1,), (1,)), ((), ()))
EXTRA = 16
CHUNKS = 4
GROUP = 16
LANES = 128


def partner_of(me, step, owners):
    total, bit = 0, 1
    while bit < owners:
        total = total + lax.rem(me // bit + step // bit, 2) * bit
        bit *= 2
    return total


def fold(extra):
    parts = extra.shape[1] // LANES
    pieces = [extra[0:4, k * LANES : (k + 1) * LANES] for k in range(parts)]
    if parts < 4:
        pieces.append(jnp.zeros((EXTRA - 4 * parts, LANES), extra.dtype))
    return jnp.concatenate(pieces, axis=0)


def unfold(folded, capacity):
    folded = folded.astype(jnp.float32)
    parts = [folded[4 * k : 4 * k + 4] for k in range(capacity // LANES)]
    return jnp.concatenate(parts, axis=1)


def weight_rows(extra):
    slots = extra.shape[1]
    row = lax.broadcasted_iota(jnp.int32, (16, slots), 0)
    kind = row % 3
    value = jnp.where(kind == 0, extra[0:1], jnp.where(kind == 1, extra[1:2], extra[2:3]))
    same = (row // 3).astype(jnp.float32) == extra[3:4]
    return jnp.where(same, value, 0.0).astype(jnp.bfloat16)


def pair_sums(bins, weights):
    slots = bins.shape[1]
    bf = jnp.bfloat16
    high = jnp.floor(bins * (1.0 / 64.0))
    low = (bins - 64.0 * high).astype(bf)
    high = high.astype(bf)
    level = lax.broadcasted_iota(jnp.int32, (16, slots), 0).astype(jnp.float32).astype(bf)
    one, zero = jnp.ones((), bf), jnp.zeros((), bf)
    lane = lax.broadcasted_iota(jnp.int32, (64, 128), 1)
    pairs = []
    for base in range(0, GROUP, 4):
        left, right = [], []
        for f in range(base, base + 4):
            high_f = jnp.broadcast_to(high[f : f + 1], (16, slots))
            low_f = jnp.broadcast_to(low[f : f + 1], (16, slots))
            for c in range(4):
                left.append(jnp.where(high_f == jnp.asarray(c, bf), weights, zero))
                right.append(jnp.where(low_f == level + jnp.asarray(16 * c, bf), one, zero))
        left = jnp.concatenate(left, axis=0)
        right = jnp.concatenate(right, axis=0)
        sums = lax.dot_general(left, right, NT, preferred_element_type=jnp.float32)
        for i in range(2):
            even = sums[128 * i : 128 * i + 64, 128 * i : 128 * i + 128]
            odd = sums[128 * i + 64 : 128 * i + 128, 128 * i : 128 * i + 128]
            pairs.append(jnp.where(lane < 64, even, odd))
    return pairs


def exchange_kernel(
    owners,
    feat_devs,
    node_count,
    capacity,
    bins_hbm,
    node_hbm,
    weight_hbm,
    treat_hbm,
    result_hbm,
    root_feat_hbm,
    root_cut_hbm,
    child_feat_hbm,
    child_cut_hbm,
    late_ref,
    late_extra_ref,
    acc_ref,
    bins_in,
    node_in,
    weight_in,
    treat_in,
    result_in,
    root_feat_in,
    root_cut_in,
    child_feat_in,
    child_cut_in,
    pick_send,
    pick_recv,
    blocks,
    extra_blocks,
    got,
    got_extra,
    bins_rows,
    extra_rows,
    slot_ref,
    places,
    weights_ref,
    in_sem,
    pick_send_sem,
    pick_recv_sem,
    send_sem,
    recv_sem,
    extra_send_sem,
    extra_recv_sem,
):
    feat_here, rows_here = bins_in.shape
    me = lax.axis_index("rows")
    mine = lax.axis_index("feat")
    bf = jnp.bfloat16

    pairs = [
        (node_hbm, node_in),
        (bins_hbm, bins_in),
        (root_feat_hbm, root_feat_in),
        (child_feat_hbm, child_feat_in),
        (root_cut_hbm, root_cut_in),
        (child_cut_hbm, child_cut_in),
        (weight_hbm, weight_in),
        (treat_hbm, treat_in),
        (result_hbm, result_in),
    ]
    loads = [pltpu.make_async_copy(a, b, in_sem.at[k]) for k, (a, b) in enumerate(pairs)]
    for load in loads:
        load.start()

    barrier = pltpu.get_barrier_semaphore()
    for step in range(1, owners):
        pl.semaphore_signal(
            barrier,
            inc=1,
            device_id={"rows": partner_of(me, step, owners)},
            device_id_type=MESH,
        )
    for step in range(1, feat_devs):
        pl.semaphore_signal(
            barrier, inc=1, device_id={"feat": lax.rem(mine + step, feat_devs)}, device_id_type=MESH
        )

    for load in loads:
        load.wait()
    node = node_in[...]
    bins = bins_in[...].astype(jnp.float32).astype(bf)
    bins_rows[...] = bins
    chosen = lax.broadcasted_iota(jnp.int32, (node_count, rows_here), 0) == node

    def column(table, stride, first):
        width = table.shape[1]
        spot = lax.broadcasted_iota(jnp.int32, (node_count, width), 0) * stride + first
        lane = lax.broadcasted_iota(jnp.int32, (node_count, width), 1)
        picked = jnp.where(lane == spot, table.astype(jnp.float32), 0.0)
        return jnp.sum(picked, axis=1, keepdims=True)

    wanted = [
        column(root_feat_in[...], 1, 0),
        column(child_feat_in[...], 2, 0),
        column(child_feat_in[...], 2, 1),
    ]
    limits = [
        column(root_cut_in[...], 1, 0),
        column(child_cut_in[...], 2, 0),
        column(child_cut_in[...], 2, 1),
    ]
    local = lax.broadcasted_iota(jnp.int32, (node_count, feat_here), 1) + mine * feat_here
    local = local.astype(jnp.float32)
    pick = jnp.concatenate([jnp.where(local == w, 1.0, 0.0) for w in wanted], axis=0).astype(bf)
    table = jnp.dot(pick, bins, preferred_element_type=jnp.float32)
    picks, cuts = [], []
    for kind in range(3):
        part = table[kind * node_count : (kind + 1) * node_count]
        picks.append(jnp.sum(jnp.where(chosen, part, 0.0), axis=0, keepdims=True))
        limit = jnp.broadcast_to(limits[kind], (node_count, rows_here))
        cuts.append(jnp.sum(jnp.where(chosen, limit, 0.0), axis=0, keepdims=True))
    picks.append(jnp.zeros_like(picks[0]))
    picks = jnp.concatenate(picks, axis=0)
    quarter = rows_here // 4
    folded = jnp.concatenate([picks[:, k * quarter : (k + 1) * quarter] for k in range(4)], axis=0)
    pick_send[...] = folded.astype(bf)

    pl.semaphore_wait(barrier, owners - 1 + feat_devs - 1)

    pick_copies = []
    for step in range(1, feat_devs):
        copy = pltpu.make_async_remote_copy(
            src_ref=pick_send,
            dst_ref=pick_recv.at[step - 1],
            send_sem=pick_send_sem.at[step - 1],
            recv_sem=pick_recv_sem.at[step - 1],
            device_id={"feat": lax.rem(mine + step, feat_devs)},
            device_id_type=MESH,
        )
        copy.start()
        pick_copies.append(copy)

    chunk = 256
    ones = chosen.astype(jnp.float32)
    up_to = lax.broadcasted_iota(jnp.int32, (chunk, chunk), 0) <= lax.broadcasted_iota(
        jnp.int32, (chunk, chunk), 1
    )
    up_to = up_to.astype(jnp.float32).astype(bf)
    before = jnp.zeros((node_count, 1), jnp.float32)
    ranks = []
    for k in range(rows_here // chunk):
        here = ones[:, k * chunk : (k + 1) * chunk]
        counts = jnp.dot(here.astype(bf), up_to, preferred_element_type=jnp.float32) + before
        ranks.append(jnp.sum(here * counts, axis=0, keepdims=True))
        before = before + jnp.sum(here, axis=1, keepdims=True)
    rank = jnp.concatenate(ranks, axis=1).astype(jnp.int32) - 1
    slot_ref[...] = node * capacity + rank

    half = owners // 2
    per = owners // CHUNKS
    late_first = owners - per
    block = min(256, capacity)
    level = lax.broadcasted_iota(jnp.int32, (16, rows_here), 0).astype(jnp.float32).astype(bf)
    one, zero = jnp.ones((), bf), jnp.zeros((), bf)

    def fill(step, where):
        target = slot_ref[...] - partner_of(me, step, owners) * capacity
        for start in range(0, capacity, block):
            inside = target - start
            inside = jnp.where((inside >= 0) & (inside < block), inside, -1)
            inside = inside.astype(jnp.float32).astype(bf)
            inside = jnp.broadcast_to(inside, (16, rows_here))
            for k in range(0, block, 16):
                places[where, start + k : start + k + 16] = jnp.where(
                    inside == level + jnp.asarray(k, bf), one, zero
                )

    def moved(rows_ref, where):
        return lax.dot_general(
            rows_ref[...], places[where], NT, preferred_element_type=jnp.float32
        )

    def send(step, late):
        return pltpu.make_async_remote_copy(
            src_ref=blocks.at[step],
            dst_ref=late_ref.at[step - late_first] if late else got.at[step],
            send_sem=send_sem.at[step],
            recv_sem=recv_sem.at[step],
            device_id={"rows": partner_of(me, step, owners)},
            device_id_type=MESH,
        )

    def send_extra(step, late):
        return pltpu.make_async_remote_copy(
            src_ref=extra_blocks.at[step],
            dst_ref=late_extra_ref.at[step - late_first] if late else got_extra.at[step],
            send_sem=extra_send_sem.at[step],
            recv_sem=extra_recv_sem.at[step],
            device_id={"rows": partner_of(me, step, owners)},
            device_id_type=MESH,
        )

    for start, stop, late in ((half, late_first, False), (late_first, owners, True)):

        @pl.loop(start, stop)
        def _(step):
            fill(step, step - half)
            blocks[step] = moved(bins_rows, step - half).astype(bf)
            send(step, late).start()

    weight, treat, result = weight_in[...], treat_in[...], result_in[...]
    scaled = weight * treat
    for copy in pick_copies:
        copy.wait()
    total = folded
    for step in range(feat_devs - 1):
        total = total + pick_recv[step].astype(jnp.float32)
    split = jnp.concatenate([total[4 * k : 4 * k + 4] for k in range(4)], axis=1)
    right_root = split[0:1] > cuts[0]
    first = jnp.where(split[1:2] > cuts[1], 1.0, 0.0)
    second = jnp.where(split[2:3] > cuts[2], 1.0, 0.0)
    leaf = jnp.where(right_root, 2.0 + second, first)
    none = jnp.zeros((EXTRA - 4, rows_here), jnp.float32)
    extra = jnp.concatenate([weight, scaled * treat, scaled * result, leaf, none], axis=0)
    extra_rows[...] = extra.astype(bf)

    for start, stop, late in ((half, late_first, False), (late_first, owners, True)):

        @pl.loop(start, stop)
        def _(step):
            extra_blocks[step] = fold(moved(extra_rows, step - half)).astype(bf)
            send_extra(step, late).start()

    @pl.loop(1, half)
    def _(back):
        step = half - back
        fill(step, step)
        blocks[step] = moved(bins_rows, step).astype(bf)
        send(step, False).start()
        extra_blocks[step] = fold(moved(extra_rows, step)).astype(bf)
        send_extra(step, False).start()

    fill(0, 0)
    got[0] = moved(bins_rows, 0).astype(bf)
    got_extra[0] = fold(moved(extra_rows, 0)).astype(bf)

    for c in range(CHUNKS - 1):
        for step in range(max(1, c * per), (c + 1) * per):
            send(step, False).wait_recv()
            send_extra(step, False).wait_recv()
        known = [unfold(got_extra[c * per + s], capacity) for s in range(per)]
        known = jnp.concatenate(known, axis=1)
        weights_ref[...] = weight_rows(known)

        @pl.loop(0, feat_here // GROUP)
        def _(block):
            rows = pl.ds(pl.multiple_of(block * GROUP, GROUP), GROUP)
            values = jnp.concatenate([got[c * per + s, rows] for s in range(per)], axis=1)
            sums = pair_sums(values.astype(jnp.float32), weights_ref[...])
            for k, part in enumerate(sums):
                spot = block * (GROUP // 2) + k
                acc_ref[spot] = part if c == 0 else acc_ref[spot] + part

    for step in range(1, owners):
        send(step, step >= late_first).wait_send()
        send_extra(step, step >= late_first).wait_send()
    for step in range(late_first, owners):
        send(step, True).wait_recv()
        send_extra(step, True).wait_recv()


def finish_kernel(late_ref, extra_ref, acc_ref, node_out, child_out, leaf_out, whole):
    sources, group, capacity = late_ref.shape
    extra = [unfold(extra_ref[s], capacity) for s in range(sources)]
    extra = jnp.concatenate(extra, axis=1)
    bins = jnp.concatenate([late_ref[s] for s in range(sources)], axis=1).astype(jnp.float32)
    lane = lax.broadcasted_iota(jnp.int32, (16, 128), 1)
    for k, part in enumerate(pair_sums(bins, weight_rows(extra))):
        part = part + acc_ref[k]
        parts = [part[16 * c : 16 * c + 16] for c in range(4)]
        turned = [pltpu.roll(p, 64, 1) for p in parts]
        for i in range(2):
            f = 2 * k + i
            for t in range(2):
                if i == 0:
                    full = jnp.where(lane < 64, parts[2 * t], turned[2 * t + 1])
                else:
                    full = jnp.where(lane < 64, turned[2 * t], parts[2 * t + 1])
                whole[t, 16 * f : 16 * f + 16] = full
    for t in range(2):
        lanes = slice(128 * t, 128 * t + 128)
        for m in range(3):
            leaves = []
            for q in range(4):
                leaf = whole[t, pl.ds(3 * q + m, group, stride=16)]
                leaf_out[q, m, :, lanes] = leaf
                leaves.append(leaf)
            left, right = leaves[0] + leaves[1], leaves[2] + leaves[3]
            child_out[0, m, :, lanes] = left
            child_out[1, m, :, lanes] = right
            node_out[0, m, :, lanes] = left + right


def on_device(
    owners,
    feat_devs,
    binned,
    node_index,
    treatment,
    outcome,
    unit_weight,
    root_feature,
    root_cutoff,
    child_feature,
    child_cutoff,
):
    rows_here, feat_here = binned.shape
    node_count = root_feature.shape[0]
    assert node_count == owners and owners >= 2 * CHUNKS and owners & (owners - 1) == 0
    capacity = 2 * rows_here // node_count
    bf, f32, i32 = jnp.bfloat16, jnp.float32, jnp.int32
    per = owners // CHUNKS
    dma = pltpu.SemaphoreType.DMA
    anywhere = pl.BlockSpec(memory_space=pltpu.HBM)
    vmem = pl.BlockSpec(memory_space=pltpu.VMEM)
    late, late_extra, acc = pl.pallas_call(
        functools.partial(exchange_kernel, owners, feat_devs, node_count, capacity),
        out_shape=(
            jax.ShapeDtypeStruct((per, feat_here, capacity), bf),
            jax.ShapeDtypeStruct((per, EXTRA, LANES), bf),
            jax.ShapeDtypeStruct((feat_here // 2, 64, 128), f32),
        ),
        in_specs=[anywhere] * 9,
        out_specs=(anywhere, anywhere, vmem),
        scratch_shapes=[
            pltpu.VMEM((feat_here, rows_here), i32),
            pltpu.VMEM((1, rows_here), i32),
            pltpu.VMEM((1, rows_here), f32),
            pltpu.VMEM((1, rows_here), f32),
            pltpu.VMEM((1, rows_here), f32),
            pltpu.VMEM((1, node_count), i32),
            pltpu.VMEM((1, node_count), i32),
            pltpu.VMEM((1, 2 * node_count), i32),
            pltpu.VMEM((1, 2 * node_count), i32),
            pltpu.VMEM((16, rows_here // 4), bf),
            pltpu.VMEM((feat_devs - 1, 16, rows_here // 4), bf),
            pltpu.VMEM((owners, feat_here, capacity), bf),
            pltpu.VMEM((owners, EXTRA, LANES), bf),
            pltpu.VMEM((owners - per, feat_here, capacity), bf),
            pltpu.VMEM((owners - per, EXTRA, LANES), bf),
            pltpu.VMEM((feat_here, rows_here), bf),
            pltpu.VMEM((EXTRA, rows_here), bf),
            pltpu.VMEM((1, rows_here), i32),
            pltpu.VMEM((owners // 2, capacity, rows_here), bf),
            pltpu.VMEM((16, per * capacity), bf),
            dma((9,)),
            dma((feat_devs - 1,)),
            dma((feat_devs - 1,)),
            dma((owners,)),
            dma((owners,)),
            dma((owners,)),
            dma((owners,)),
        ],
        compiler_params=pltpu.CompilerParams(
            collective_id=0, has_side_effects=True, vmem_limit_bytes=64 * 1024 * 1024
        ),
        name="exchange",
    )(
        binned.T,
        node_index.reshape(1, rows_here),
        unit_weight.reshape(1, rows_here),
        treatment.reshape(1, rows_here),
        outcome.reshape(1, rows_here),
        root_feature.reshape(1, node_count),
        root_cutoff.reshape(1, node_count),
        child_feature.reshape(1, 2 * node_count),
        child_cutoff.reshape(1, 2 * node_count),
    )

    return pl.pallas_call(
        finish_kernel,
        grid=(feat_here // GROUP,),
        out_shape=tuple(
            jax.ShapeDtypeStruct((k, 3, feat_here, BINS), f32) for k in (1, 2, 4)
        ),
        in_specs=[
            pl.BlockSpec((per, GROUP, capacity), lambda i: (0, i, 0)),
            pl.BlockSpec((per, EXTRA, LANES), lambda i: (0, 0, 0)),
            pl.BlockSpec((GROUP // 2, 64, 128), lambda i: (i, 0, 0)),
        ],
        out_specs=tuple(pl.BlockSpec((k, 3, GROUP, BINS), lambda i: (0, 0, i, 0)) for k in (1, 2, 4)),
        scratch_shapes=[pltpu.VMEM((2, GROUP * 16, 128), f32)],
        compiler_params=pltpu.CompilerParams(vmem_limit_bytes=64 * 1024 * 1024),
        name="finish",
    )(late, late_extra, acc)


def solution(mesh):
    in_specs = (
        P("rows", "feat"),
        P("rows", None),
        P("rows"),
        P("rows"),
        P("rows"),
        P(),
        P(),
        P(),
        P(),
    )
    out_specs = (P("rows", None, "feat", None),) * 3
    body = functools.partial(on_device, mesh.shape["rows"], mesh.shape["feat"])
    return jax.shard_map(body, mesh=mesh, in_specs=in_specs, out_specs=out_specs, check_vma=False)
```

```python
import functools

import jax
import jax.numpy as jnp
from jax import lax
from jax.experimental import pallas as pl
from jax.experimental.pallas import tpu as pltpu
from jax.sharding import PartitionSpec as P

BINS = 256
MESH = pl.DeviceIdType.MESH
NT = (((1,), (1,)), ((), ()))
EXTRA = 16
CHUNKS = 4
GROUP = 16
LANES = 128


def partner_of(me, step, owners):
    total, bit = 0, 1
    while bit < owners:
        total = total + lax.rem(me // bit + step // bit, 2) * bit
        bit *= 2
    return total


def fold(extra):
    parts = extra.shape[1] // LANES
    pieces = [extra[0:4, k * LANES : (k + 1) * LANES] for k in range(parts)]
    if parts < 4:
        pieces.append(jnp.zeros((EXTRA - 4 * parts, LANES), extra.dtype))
    return jnp.concatenate(pieces, axis=0)


def unfold(folded, capacity):
    folded = folded.astype(jnp.float32)
    parts = [folded[4 * k : 4 * k + 4] for k in range(capacity // LANES)]
    return jnp.concatenate(parts, axis=1)


def weight_rows(extra):
    slots = extra.shape[1]
    row = lax.broadcasted_iota(jnp.int32, (16, slots), 0)
    kind = row % 3
    value = jnp.where(kind == 0, extra[0:1], jnp.where(kind == 1, extra[1:2], extra[2:3]))
    same = (row // 3).astype(jnp.float32) == extra[3:4]
    return jnp.where(same, value, 0.0).astype(jnp.bfloat16)


def group_sums(high_ref, low_ref, group, weights):
    slots = high_ref.shape[1]
    bf = jnp.bfloat16
    level = lax.broadcasted_iota(jnp.int32, (16, slots), 0).astype(jnp.float32).astype(bf)
    one, zero = jnp.ones((), bf), jnp.zeros((), bf)
    left, right = [], []
    for i in range(4):
        row = pl.ds(4 * group + i, 1)
        high = jnp.broadcast_to(high_ref[row], (16, slots)).astype(bf)
        low = jnp.broadcast_to(low_ref[row], (16, slots)).astype(bf)
        for c in range(4):
            left.append(jnp.where(high == jnp.asarray(c, bf), weights, zero))
            right.append(jnp.where(low == level + jnp.asarray(16 * c, bf), one, zero))
    left = jnp.concatenate(left, axis=0)
    right = jnp.concatenate(right, axis=0)
    sums = lax.dot_general(left, right, NT, preferred_element_type=jnp.float32)
    lane = lax.broadcasted_iota(jnp.int32, (64, 128), 1)
    pairs = []
    for i in range(2):
        even = sums[128 * i : 128 * i + 64, 128 * i : 128 * i + 128]
        odd = sums[128 * i + 64 : 128 * i + 128, 128 * i : 128 * i + 128]
        pairs.append(jnp.where(lane < 64, even, odd))
    return pairs


def exchange_kernel(
    owners,
    feat_devs,
    node_count,
    capacity,
    bins_hbm,
    node_hbm,
    weight_hbm,
    treat_hbm,
    result_hbm,
    root_feat_hbm,
    root_cut_hbm,
    child_feat_hbm,
    child_cut_hbm,
    acc_ref,
    bins_in,
    node_in,
    weight_in,
    treat_in,
    result_in,
    root_feat_in,
    root_cut_in,
    child_feat_in,
    child_cut_in,
    pick_send,
    pick_recv,
    blocks,
    extra_blocks,
    got,
    got_extra,
    bins_rows,
    extra_rows,
    slot_ref,
    places,
    weights_ref,
    high_ref,
    low_ref,
    in_sem,
    pick_send_sem,
    pick_recv_sem,
    send_sem,
    recv_sem,
    extra_send_sem,
    extra_recv_sem,
):
    feat_here, rows_here = bins_in.shape
    me = lax.axis_index("rows")
    mine = lax.axis_index("feat")
    bf = jnp.bfloat16

    pairs = [
        (node_hbm, node_in),
        (bins_hbm, bins_in),
        (root_feat_hbm, root_feat_in),
        (child_feat_hbm, child_feat_in),
        (root_cut_hbm, root_cut_in),
        (child_cut_hbm, child_cut_in),
        (weight_hbm, weight_in),
        (treat_hbm, treat_in),
        (result_hbm, result_in),
    ]
    loads = [pltpu.make_async_copy(a, b, in_sem.at[k]) for k, (a, b) in enumerate(pairs)]
    for load in loads:
        load.start()

    barrier = pltpu.get_barrier_semaphore()
    for step in range(1, owners):
        pl.semaphore_signal(
            barrier,
            inc=1,
            device_id={"rows": partner_of(me, step, owners)},
            device_id_type=MESH,
        )
    for step in range(1, feat_devs):
        pl.semaphore_signal(
            barrier, inc=1, device_id={"feat": lax.rem(mine + step, feat_devs)}, device_id_type=MESH
        )

    for load in loads:
        load.wait()
    node = node_in[...]
    bins = bins_in[...].astype(jnp.float32).astype(bf)
    bins_rows[...] = bins
    chosen = lax.broadcasted_iota(jnp.int32, (node_count, rows_here), 0) == node

    def column(table, stride, first):
        width = table.shape[1]
        spot = lax.broadcasted_iota(jnp.int32, (node_count, width), 0) * stride + first
        lane = lax.broadcasted_iota(jnp.int32, (node_count, width), 1)
        picked = jnp.where(lane == spot, table.astype(jnp.float32), 0.0)
        return jnp.sum(picked, axis=1, keepdims=True)

    wanted = [
        column(root_feat_in[...], 1, 0),
        column(child_feat_in[...], 2, 0),
        column(child_feat_in[...], 2, 1),
    ]
    limits = [
        column(root_cut_in[...], 1, 0),
        column(child_cut_in[...], 2, 0),
        column(child_cut_in[...], 2, 1),
    ]
    local = lax.broadcasted_iota(jnp.int32, (node_count, feat_here), 1) + mine * feat_here
    local = local.astype(jnp.float32)
    pick = jnp.concatenate([jnp.where(local == w, 1.0, 0.0) for w in wanted], axis=0).astype(bf)
    table = jnp.dot(pick, bins, preferred_element_type=jnp.float32)
    picks, cuts = [], []
    for kind in range(3):
        part = table[kind * node_count : (kind + 1) * node_count]
        picks.append(jnp.sum(jnp.where(chosen, part, 0.0), axis=0, keepdims=True))
        limit = jnp.broadcast_to(limits[kind], (node_count, rows_here))
        cuts.append(jnp.sum(jnp.where(chosen, limit, 0.0), axis=0, keepdims=True))
    picks.append(jnp.zeros_like(picks[0]))
    picks = jnp.concatenate(picks, axis=0)
    quarter = rows_here // 4
    folded = jnp.concatenate([picks[:, k * quarter : (k + 1) * quarter] for k in range(4)], axis=0)
    pick_send[...] = folded.astype(bf)

    pl.semaphore_wait(barrier, owners - 1 + feat_devs - 1)

    pick_copies = []
    for step in range(1, feat_devs):
        copy = pltpu.make_async_remote_copy(
            src_ref=pick_send,
            dst_ref=pick_recv.at[step - 1],
            send_sem=pick_send_sem.at[step - 1],
            recv_sem=pick_recv_sem.at[step - 1],
            device_id={"feat": lax.rem(mine + step, feat_devs)},
            device_id_type=MESH,
        )
        copy.start()
        pick_copies.append(copy)

    chunk = 256
    ones = chosen.astype(jnp.float32)
    up_to = lax.broadcasted_iota(jnp.int32, (chunk, chunk), 0) <= lax.broadcasted_iota(
        jnp.int32, (chunk, chunk), 1
    )
    up_to = up_to.astype(jnp.float32).astype(bf)
    before = jnp.zeros((node_count, 1), jnp.float32)
    ranks = []
    for k in range(rows_here // chunk):
        here = ones[:, k * chunk : (k + 1) * chunk]
        counts = jnp.dot(here.astype(bf), up_to, preferred_element_type=jnp.float32) + before
        ranks.append(jnp.sum(here * counts, axis=0, keepdims=True))
        before = before + jnp.sum(here, axis=1, keepdims=True)
    rank = jnp.concatenate(ranks, axis=1).astype(jnp.int32) - 1
    slot_ref[...] = node * capacity + rank

    half = owners // 2
    per = owners // CHUNKS
    block = min(256, capacity)
    level = lax.broadcasted_iota(jnp.int32, (16, rows_here), 0).astype(jnp.float32).astype(bf)
    one, zero = jnp.ones((), bf), jnp.zeros((), bf)

    def fill(step, where):
        target = slot_ref[...] - partner_of(me, step, owners) * capacity

        @pl.loop(0, capacity // block)
        def _(part):
            inside = target - part * block
            inside = jnp.where((inside >= 0) & (inside < block), inside, -1)
            inside = inside.astype(jnp.float32).astype(bf)
            inside = jnp.broadcast_to(inside, (16, rows_here))
            for k in range(0, block, 16):
                rows = pl.ds(pl.multiple_of(part * block + k, 16), 16)
                places[where, rows] = jnp.where(inside == level + jnp.asarray(k, bf), one, zero)

    def moved(rows_ref, where):
        return lax.dot_general(
            rows_ref[...], places[where], NT, preferred_element_type=jnp.float32
        )

    def send(step):
        return pltpu.make_async_remote_copy(
            src_ref=blocks.at[step],
            dst_ref=got.at[step],
            send_sem=send_sem.at[step],
            recv_sem=recv_sem.at[step],
            device_id={"rows": partner_of(me, step, owners)},
            device_id_type=MESH,
        )

    def send_extra(step):
        return pltpu.make_async_remote_copy(
            src_ref=extra_blocks.at[step],
            dst_ref=got_extra.at[step],
            send_sem=extra_send_sem.at[step],
            recv_sem=extra_recv_sem.at[step],
            device_id={"rows": partner_of(me, step, owners)},
            device_id_type=MESH,
        )

    @pl.loop(half, owners)
    def _(step):
        fill(step, step - half)
        blocks[step] = moved(bins_rows, step - half).astype(bf)
        send(step).start()

    weight, treat, result = weight_in[...], treat_in[...], result_in[...]
    scaled = weight * treat
    for copy in pick_copies:
        copy.wait()
    total = folded
    for step in range(feat_devs - 1):
        total = total + pick_recv[step].astype(jnp.float32)
    split = jnp.concatenate([total[4 * k : 4 * k + 4] for k in range(4)], axis=1)
    right_root = split[0:1] > cuts[0]
    first = jnp.where(split[1:2] > cuts[1], 1.0, 0.0)
    second = jnp.where(split[2:3] > cuts[2], 1.0, 0.0)
    leaf = jnp.where(right_root, 2.0 + second, first)
    none = jnp.zeros((EXTRA - 4, rows_here), jnp.float32)
    extra = jnp.concatenate([weight, scaled * treat, scaled * result, leaf, none], axis=0)
    extra_rows[...] = extra.astype(bf)

    @pl.loop(0, half)
    def _(back):
        far, near = owners - 1 - back, half - 1 - back
        extra_blocks[far] = fold(moved(extra_rows, near)).astype(bf)
        send_extra(far).start()
        fill(near, near)
        blocks[near] = moved(bins_rows, near).astype(bf)
        extra_blocks[near] = fold(moved(extra_rows, near)).astype(bf)

        @pl.when(near > 0)
        def _():
            send(near).start()
            send_extra(near).start()

    got[0] = blocks[0]
    got_extra[0] = extra_blocks[0]
    acc_ref[...] = jnp.zeros_like(acc_ref)

    @pl.loop(0, CHUNKS)
    def _(c):
        for s in range(per):
            step = c * per + s

            @pl.when(step > 0)
            def _():
                send(step).wait_recv()
                send_extra(step).wait_recv()

        known = [unfold(got_extra[c * per + s], capacity) for s in range(per)]
        weights_ref[...] = weight_rows(jnp.concatenate(known, axis=1))
        for s in range(per):
            bins = got[c * per + s].astype(jnp.float32)
            high = jnp.floor(bins * (1.0 / 64.0))
            high_ref[:, s * capacity : (s + 1) * capacity] = high
            low_ref[:, s * capacity : (s + 1) * capacity] = bins - 64.0 * high

        @pl.loop(0, feat_here // 4)
        def _(group):
            for k, part in enumerate(group_sums(high_ref, low_ref, group, weights_ref[...])):
                acc_ref[2 * group + k] += part

    @pl.loop(1, owners)
    def _(step):
        send(step).wait_send()
        send_extra(step).wait_send()


def finish_kernel(acc_ref, node_out, child_out, leaf_out, whole):
    lane = lax.broadcasted_iota(jnp.int32, (16, 128), 1)
    group = 2 * acc_ref.shape[0]
    for k in range(group // 2):
        part = acc_ref[k]
        parts = [part[16 * c : 16 * c + 16] for c in range(4)]
        turned = [pltpu.roll(p, 64, 1) for p in parts]
        for i in range(2):
            f = 2 * k + i
            for t in range(2):
                if i == 0:
                    full = jnp.where(lane < 64, parts[2 * t], turned[2 * t + 1])
                else:
                    full = jnp.where(lane < 64, turned[2 * t], parts[2 * t + 1])
                whole[t, 16 * f : 16 * f + 16] = full
    for t in range(2):
        lanes = slice(128 * t, 128 * t + 128)
        for m in range(3):
            leaves = []
            for q in range(4):
                leaf = whole[t, pl.ds(3 * q + m, group, stride=16)]
                leaf_out[q, m, :, lanes] = leaf
                leaves.append(leaf)
            left, right = leaves[0] + leaves[1], leaves[2] + leaves[3]
            child_out[0, m, :, lanes] = left
            child_out[1, m, :, lanes] = right
            node_out[0, m, :, lanes] = left + right


def on_device(
    owners,
    feat_devs,
    binned,
    node_index,
    treatment,
    outcome,
    unit_weight,
    root_feature,
    root_cutoff,
    child_feature,
    child_cutoff,
):
    rows_here, feat_here = binned.shape
    node_count = root_feature.shape[0]
    assert node_count == owners and owners >= 2 * CHUNKS and owners & (owners - 1) == 0
    capacity = 2 * rows_here // node_count
    bf, f32, i32 = jnp.bfloat16, jnp.float32, jnp.int32
    per = owners // CHUNKS
    dma = pltpu.SemaphoreType.DMA
    anywhere = pl.BlockSpec(memory_space=pltpu.HBM)
    vmem = pl.BlockSpec(memory_space=pltpu.VMEM)
    acc = pl.pallas_call(
        functools.partial(exchange_kernel, owners, feat_devs, node_count, capacity),
        out_shape=jax.ShapeDtypeStruct((feat_here // 2, 64, 128), f32),
        in_specs=[anywhere] * 9,
        out_specs=vmem,
        scratch_shapes=[
            pltpu.VMEM((feat_here, rows_here), i32),
            pltpu.VMEM((1, rows_here), i32),
            pltpu.VMEM((1, rows_here), f32),
            pltpu.VMEM((1, rows_here), f32),
            pltpu.VMEM((1, rows_here), f32),
            pltpu.VMEM((1, node_count), i32),
            pltpu.VMEM((1, node_count), i32),
            pltpu.VMEM((1, 2 * node_count), i32),
            pltpu.VMEM((1, 2 * node_count), i32),
            pltpu.VMEM((16, rows_here // 4), bf),
            pltpu.VMEM((feat_devs - 1, 16, rows_here // 4), bf),
            pltpu.VMEM((owners, feat_here, capacity), bf),
            pltpu.VMEM((owners, EXTRA, LANES), bf),
            pltpu.VMEM((owners, feat_here, capacity), bf),
            pltpu.VMEM((owners, EXTRA, LANES), bf),
            pltpu.VMEM((feat_here, rows_here), bf),
            pltpu.VMEM((EXTRA, rows_here), bf),
            pltpu.VMEM((1, rows_here), i32),
            pltpu.VMEM((owners // 2, capacity, rows_here), bf),
            pltpu.VMEM((16, per * capacity), bf),
            pltpu.VMEM((feat_here, per * capacity), f32),
            pltpu.VMEM((feat_here, per * capacity), f32),
            dma((9,)),
            dma((feat_devs - 1,)),
            dma((feat_devs - 1,)),
            dma((owners,)),
            dma((owners,)),
            dma((owners,)),
            dma((owners,)),
        ],
        compiler_params=pltpu.CompilerParams(
            collective_id=0, has_side_effects=True, vmem_limit_bytes=64 * 1024 * 1024
        ),
        name="exchange",
    )(
        binned.T,
        node_index.reshape(1, rows_here),
        unit_weight.reshape(1, rows_here),
        treatment.reshape(1, rows_here),
        outcome.reshape(1, rows_here),
        root_feature.reshape(1, node_count),
        root_cutoff.reshape(1, node_count),
        child_feature.reshape(1, 2 * node_count),
        child_cutoff.reshape(1, 2 * node_count),
    )

    return pl.pallas_call(
        finish_kernel,
        grid=(feat_here // GROUP,),
        out_shape=tuple(
            jax.ShapeDtypeStruct((k, 3, feat_here, BINS), f32) for k in (1, 2, 4)
        ),
        in_specs=[
            pl.BlockSpec((GROUP // 2, 64, 128), lambda i: (i, 0, 0)),
        ],
        out_specs=tuple(pl.BlockSpec((k, 3, GROUP, BINS), lambda i: (0, 0, i, 0)) for k in (1, 2, 4)),
        scratch_shapes=[pltpu.VMEM((2, GROUP * 16, 128), f32)],
        compiler_params=pltpu.CompilerParams(vmem_limit_bytes=64 * 1024 * 1024),
        name="finish",
    )(acc)


def solution(mesh):
    in_specs = (
        P("rows", "feat"),
        P("rows", None),
        P("rows"),
        P("rows"),
        P("rows"),
        P(),
        P(),
        P(),
        P(),
    )
    out_specs = (P("rows", None, "feat", None),) * 3
    body = functools.partial(on_device, mesh.shape["rows"], mesh.shape["feat"])
    return jax.shard_map(body, mesh=mesh, in_specs=in_specs, out_specs=out_specs, check_vma=False)
```

```python
import functools

import jax
import jax.numpy as jnp
from jax import lax
from jax.experimental import pallas as pl
from jax.experimental.pallas import tpu as pltpu
from jax.sharding import PartitionSpec as P

BINS = 256
MESH = pl.DeviceIdType.MESH
NT = (((1,), (1,)), ((), ()))
EXTRA = 16
CHUNKS = 4
GROUP = 16
LANES = 128


def partner_of(me, step, owners):
    total, bit = 0, 1
    while bit < owners:
        total = total + lax.rem(me // bit + step // bit, 2) * bit
        bit *= 2
    return total


def fold(extra):
    parts = extra.shape[1] // LANES
    pieces = [extra[0:4, k * LANES : (k + 1) * LANES] for k in range(parts)]
    if parts < 4:
        pieces.append(jnp.zeros((EXTRA - 4 * parts, LANES), extra.dtype))
    return jnp.concatenate(pieces, axis=0)


def unfold(folded, capacity):
    folded = folded.astype(jnp.float32)
    parts = [folded[4 * k : 4 * k + 4] for k in range(capacity // LANES)]
    return jnp.concatenate(parts, axis=1)


def weight_rows(extra):
    slots = extra.shape[1]
    row = lax.broadcasted_iota(jnp.int32, (16, slots), 0)
    kind = row % 3
    value = jnp.where(kind == 0, extra[0:1], jnp.where(kind == 1, extra[1:2], extra[2:3]))
    same = (row // 3).astype(jnp.float32) == extra[3:4]
    return jnp.where(same, value, 0.0).astype(jnp.bfloat16)


def pair_sums(bins, weights):
    slots = bins.shape[1]
    bf = jnp.bfloat16
    high = jnp.floor(bins * (1.0 / 64.0))
    low = (bins - 64.0 * high).astype(bf)
    high = high.astype(bf)
    level = lax.broadcasted_iota(jnp.int32, (16, slots), 0).astype(jnp.float32).astype(bf)
    one, zero = jnp.ones((), bf), jnp.zeros((), bf)
    lane = lax.broadcasted_iota(jnp.int32, (64, 128), 1)
    pairs = []
    for base in range(0, GROUP, 4):
        left, right = [], []
        for f in range(base, base + 4):
            high_f = jnp.broadcast_to(high[f : f + 1], (16, slots))
            low_f = jnp.broadcast_to(low[f : f + 1], (16, slots))
            for c in range(4):
                left.append(jnp.where(high_f == jnp.asarray(c, bf), weights, zero))
                right.append(jnp.where(low_f == level + jnp.asarray(16 * c, bf), one, zero))
        left = jnp.concatenate(left, axis=0)
        right = jnp.concatenate(right, axis=0)
        sums = lax.dot_general(left, right, NT, preferred_element_type=jnp.float32)
        for i in range(2):
            even = sums[128 * i : 128 * i + 64, 128 * i : 128 * i + 128]
            odd = sums[128 * i + 64 : 128 * i + 128, 128 * i : 128 * i + 128]
            pairs.append(jnp.where(lane < 64, even, odd))
    return pairs


def exchange_kernel(
    owners,
    feat_devs,
    node_count,
    capacity,
    bins_hbm,
    node_hbm,
    weight_hbm,
    treat_hbm,
    result_hbm,
    root_feat_hbm,
    root_cut_hbm,
    child_feat_hbm,
    child_cut_hbm,
    acc_ref,
    bins_in,
    node_in,
    weight_in,
    treat_in,
    result_in,
    root_feat_in,
    root_cut_in,
    child_feat_in,
    child_cut_in,
    pick_send,
    pick_recv,
    blocks,
    extra_blocks,
    got,
    got_extra,
    rows_in,
    slot_ref,
    places,
    weights_ref,
    in_sem,
    pick_send_sem,
    pick_recv_sem,
    send_sem,
    recv_sem,
    extra_send_sem,
    extra_recv_sem,
):
    feat_here, rows_here = bins_in.shape
    me = lax.axis_index("rows")
    mine = lax.axis_index("feat")
    bf = jnp.bfloat16

    pairs = [
        (node_hbm, node_in),
        (bins_hbm, bins_in),
        (root_feat_hbm, root_feat_in),
        (child_feat_hbm, child_feat_in),
        (root_cut_hbm, root_cut_in),
        (child_cut_hbm, child_cut_in),
        (weight_hbm, weight_in),
        (treat_hbm, treat_in),
        (result_hbm, result_in),
    ]
    loads = [pltpu.make_async_copy(a, b, in_sem.at[k]) for k, (a, b) in enumerate(pairs)]
    for load in loads:
        load.start()

    barrier = pltpu.get_barrier_semaphore()
    for step in range(1, owners):
        pl.semaphore_signal(
            barrier,
            inc=1,
            device_id={"rows": partner_of(me, step, owners)},
            device_id_type=MESH,
        )
    for step in range(1, feat_devs):
        pl.semaphore_signal(
            barrier, inc=1, device_id={"feat": lax.rem(mine + step, feat_devs)}, device_id_type=MESH
        )

    for load in loads:
        load.wait()
    node = node_in[...]
    bins = bins_in[...].astype(jnp.float32).astype(bf)
    rows_in[0:feat_here] = bins
    chosen = lax.broadcasted_iota(jnp.int32, (node_count, rows_here), 0) == node

    def column(table, stride, first):
        width = table.shape[1]
        spot = lax.broadcasted_iota(jnp.int32, (node_count, width), 0) * stride + first
        lane = lax.broadcasted_iota(jnp.int32, (node_count, width), 1)
        picked = jnp.where(lane == spot, table.astype(jnp.float32), 0.0)
        return jnp.sum(picked, axis=1, keepdims=True)

    wanted = [
        column(root_feat_in[...], 1, 0),
        column(child_feat_in[...], 2, 0),
        column(child_feat_in[...], 2, 1),
    ]
    limits = [
        column(root_cut_in[...], 1, 0),
        column(child_cut_in[...], 2, 0),
        column(child_cut_in[...], 2, 1),
    ]
    local = lax.broadcasted_iota(jnp.int32, (node_count, feat_here), 1) + mine * feat_here
    local = local.astype(jnp.float32)
    pick = jnp.concatenate([jnp.where(local == w, 1.0, 0.0) for w in wanted], axis=0).astype(bf)
    table = jnp.dot(pick, bins, preferred_element_type=jnp.float32)
    picks, cuts = [], []
    for kind in range(3):
        part = table[kind * node_count : (kind + 1) * node_count]
        picks.append(jnp.sum(jnp.where(chosen, part, 0.0), axis=0, keepdims=True))
        limit = jnp.broadcast_to(limits[kind], (node_count, rows_here))
        cuts.append(jnp.sum(jnp.where(chosen, limit, 0.0), axis=0, keepdims=True))
    picks.append(jnp.zeros_like(picks[0]))
    picks = jnp.concatenate(picks, axis=0)
    quarter = rows_here // 4
    folded = jnp.concatenate([picks[:, k * quarter : (k + 1) * quarter] for k in range(4)], axis=0)
    pick_send[...] = folded.astype(bf)

    pl.semaphore_wait(barrier, owners - 1 + feat_devs - 1)

    pick_copies = []
    for step in range(1, feat_devs):
        copy = pltpu.make_async_remote_copy(
            src_ref=pick_send,
            dst_ref=pick_recv.at[step - 1],
            send_sem=pick_send_sem.at[step - 1],
            recv_sem=pick_recv_sem.at[step - 1],
            device_id={"feat": lax.rem(mine + step, feat_devs)},
            device_id_type=MESH,
        )
        copy.start()
        pick_copies.append(copy)

    chunk = 256
    ones = chosen.astype(jnp.float32)
    up_to = lax.broadcasted_iota(jnp.int32, (chunk, chunk), 0) <= lax.broadcasted_iota(
        jnp.int32, (chunk, chunk), 1
    )
    up_to = up_to.astype(jnp.float32).astype(bf)
    before = jnp.zeros((node_count, 1), jnp.float32)
    ranks = []
    for k in range(rows_here // chunk):
        here = ones[:, k * chunk : (k + 1) * chunk]
        counts = jnp.dot(here.astype(bf), up_to, preferred_element_type=jnp.float32) + before
        ranks.append(jnp.sum(here * counts, axis=0, keepdims=True))
        before = before + jnp.sum(here, axis=1, keepdims=True)
    rank = jnp.concatenate(ranks, axis=1).astype(jnp.int32) - 1
    slot_ref[...] = node * capacity + rank

    half = owners // 2
    per = owners // CHUNKS
    block = min(256, capacity)
    level = lax.broadcasted_iota(jnp.int32, (16, rows_here), 0).astype(jnp.float32).astype(bf)
    one, zero = jnp.ones((), bf), jnp.zeros((), bf)

    def fill(step, where):
        target = slot_ref[...] - partner_of(me, step, owners) * capacity

        @pl.loop(0, capacity // block)
        def _(part):
            inside = target - part * block
            inside = jnp.where((inside >= 0) & (inside < block), inside, -1)
            inside = inside.astype(jnp.float32).astype(bf)
            inside = jnp.broadcast_to(inside, (16, rows_here))
            for k in range(0, block, 16):
                rows = pl.ds(pl.multiple_of(part * block + k, 16), 16)
                places[where, rows] = jnp.where(inside == level + jnp.asarray(k, bf), one, zero)

    def pack(step, where):
        moved = lax.dot_general(rows_in[...], places[where], NT, preferred_element_type=jnp.float32)
        blocks[step] = moved[0:feat_here].astype(bf)
        extra_blocks[step] = fold(moved[feat_here : feat_here + EXTRA]).astype(bf)

    def send(step):
        return pltpu.make_async_remote_copy(
            src_ref=blocks.at[step],
            dst_ref=got.at[step],
            send_sem=send_sem.at[step],
            recv_sem=recv_sem.at[step],
            device_id={"rows": partner_of(me, step, owners)},
            device_id_type=MESH,
        )

    def send_extra(step):
        return pltpu.make_async_remote_copy(
            src_ref=extra_blocks.at[step],
            dst_ref=got_extra.at[step],
            send_sem=extra_send_sem.at[step],
            recv_sem=extra_recv_sem.at[step],
            device_id={"rows": partner_of(me, step, owners)},
            device_id_type=MESH,
        )

    @pl.loop(half, owners)
    def _(step):
        fill(step, step - half)

    weight, treat, result = weight_in[...], treat_in[...], result_in[...]
    scaled = weight * treat
    for copy in pick_copies:
        copy.wait()
    total = folded
    for step in range(feat_devs - 1):
        total = total + pick_recv[step].astype(jnp.float32)
    split = jnp.concatenate([total[4 * k : 4 * k + 4] for k in range(4)], axis=1)
    right_root = split[0:1] > cuts[0]
    first = jnp.where(split[1:2] > cuts[1], 1.0, 0.0)
    second = jnp.where(split[2:3] > cuts[2], 1.0, 0.0)
    leaf = jnp.where(right_root, 2.0 + second, first)
    none = jnp.zeros((EXTRA - 4, rows_here), jnp.float32)
    extra = jnp.concatenate([weight, scaled * treat, scaled * result, leaf, none], axis=0)
    rows_in[feat_here : feat_here + EXTRA] = extra.astype(bf)

    @pl.loop(half, owners)
    def _(step):
        pack(step, step - half)
        send(step).start()
        send_extra(step).start()

    @pl.loop(0, half)
    def _(back):
        step = half - 1 - back
        fill(step, step)
        pack(step, step)

        @pl.when(step > 0)
        def _():
            send(step).start()
            send_extra(step).start()

    got[0] = blocks[0]
    got_extra[0] = extra_blocks[0]
    acc_ref[...] = jnp.zeros_like(acc_ref)

    @pl.loop(0, CHUNKS)
    def _(c):
        for s in range(per):
            step = c * per + s

            @pl.when(step > 0)
            def _():
                send(step).wait_recv()
                send_extra(step).wait_recv()

        known = [unfold(got_extra[c * per + s], capacity) for s in range(per)]
        weights_ref[...] = weight_rows(jnp.concatenate(known, axis=1))

        @pl.loop(0, feat_here // GROUP)
        def _(part):
            rows = pl.ds(pl.multiple_of(part * GROUP, GROUP), GROUP)
            values = jnp.concatenate([got[c * per + s, rows] for s in range(per)], axis=1)
            for k, sums in enumerate(pair_sums(values.astype(jnp.float32), weights_ref[...])):
                acc_ref[part * (GROUP // 2) + k] += sums

    @pl.loop(1, owners)
    def _(step):
        send(step).wait_send()
        send_extra(step).wait_send()


def finish_kernel(acc_ref, node_out, child_out, leaf_out, whole):
    lane = lax.broadcasted_iota(jnp.int32, (16, 128), 1)
    group = 2 * acc_ref.shape[0]
    for k in range(group // 2):
        part = acc_ref[k]
        parts = [part[16 * c : 16 * c + 16] for c in range(4)]
        turned = [pltpu.roll(p, 64, 1) for p in parts]
        for i in range(2):
            f = 2 * k + i
            for t in range(2):
                if i == 0:
                    full = jnp.where(lane < 64, parts[2 * t], turned[2 * t + 1])
                else:
                    full = jnp.where(lane < 64, turned[2 * t], parts[2 * t + 1])
                whole[t, 16 * f : 16 * f + 16] = full
    for t in range(2):
        lanes = slice(128 * t, 128 * t + 128)
        for m in range(3):
            leaves = []
            for q in range(4):
                leaf = whole[t, pl.ds(3 * q + m, group, stride=16)]
                leaf_out[q, m, :, lanes] = leaf
                leaves.append(leaf)
            left, right = leaves[0] + leaves[1], leaves[2] + leaves[3]
            child_out[0, m, :, lanes] = left
            child_out[1, m, :, lanes] = right
            node_out[0, m, :, lanes] = left + right


def on_device(
    owners,
    feat_devs,
    binned,
    node_index,
    treatment,
    outcome,
    unit_weight,
    root_feature,
    root_cutoff,
    child_feature,
    child_cutoff,
):
    rows_here, feat_here = binned.shape
    node_count = root_feature.shape[0]
    assert node_count == owners and owners >= 2 * CHUNKS and owners & (owners - 1) == 0
    capacity = 2 * rows_here // node_count
    bf, f32, i32 = jnp.bfloat16, jnp.float32, jnp.int32
    per = owners // CHUNKS
    dma = pltpu.SemaphoreType.DMA
    anywhere = pl.BlockSpec(memory_space=pltpu.HBM)
    vmem = pl.BlockSpec(memory_space=pltpu.VMEM)
    acc = pl.pallas_call(
        functools.partial(exchange_kernel, owners, feat_devs, node_count, capacity),
        out_shape=jax.ShapeDtypeStruct((feat_here // 2, 64, 128), f32),
        in_specs=[anywhere] * 9,
        out_specs=vmem,
        scratch_shapes=[
            pltpu.VMEM((feat_here, rows_here), i32),
            pltpu.VMEM((1, rows_here), i32),
            pltpu.VMEM((1, rows_here), f32),
            pltpu.VMEM((1, rows_here), f32),
            pltpu.VMEM((1, rows_here), f32),
            pltpu.VMEM((1, node_count), i32),
            pltpu.VMEM((1, node_count), i32),
            pltpu.VMEM((1, 2 * node_count), i32),
            pltpu.VMEM((1, 2 * node_count), i32),
            pltpu.VMEM((16, rows_here // 4), bf),
            pltpu.VMEM((feat_devs - 1, 16, rows_here // 4), bf),
            pltpu.VMEM((owners, feat_here, capacity), bf),
            pltpu.VMEM((owners, EXTRA, LANES), bf),
            pltpu.VMEM((owners, feat_here, capacity), bf),
            pltpu.VMEM((owners, EXTRA, LANES), bf),
            pltpu.VMEM((feat_here + EXTRA, rows_here), bf),
            pltpu.VMEM((1, rows_here), i32),
            pltpu.VMEM((owners // 2, capacity, rows_here), bf),
            pltpu.VMEM((16, per * capacity), bf),
            dma((9,)),
            dma((feat_devs - 1,)),
            dma((feat_devs - 1,)),
            dma((owners,)),
            dma((owners,)),
            dma((owners,)),
            dma((owners,)),
        ],
        compiler_params=pltpu.CompilerParams(
            collective_id=0, has_side_effects=True, vmem_limit_bytes=64 * 1024 * 1024
        ),
        name="exchange",
    )(
        binned.T,
        node_index.reshape(1, rows_here),
        unit_weight.reshape(1, rows_here),
        treatment.reshape(1, rows_here),
        outcome.reshape(1, rows_here),
        root_feature.reshape(1, node_count),
        root_cutoff.reshape(1, node_count),
        child_feature.reshape(1, 2 * node_count),
        child_cutoff.reshape(1, 2 * node_count),
    )

    return pl.pallas_call(
        finish_kernel,
        grid=(feat_here // GROUP,),
        out_shape=tuple(
            jax.ShapeDtypeStruct((k, 3, feat_here, BINS), f32) for k in (1, 2, 4)
        ),
        in_specs=[
            pl.BlockSpec((GROUP // 2, 64, 128), lambda i: (i, 0, 0)),
        ],
        out_specs=tuple(pl.BlockSpec((k, 3, GROUP, BINS), lambda i: (0, 0, i, 0)) for k in (1, 2, 4)),
        scratch_shapes=[pltpu.VMEM((2, GROUP * 16, 128), f32)],
        compiler_params=pltpu.CompilerParams(vmem_limit_bytes=64 * 1024 * 1024),
        name="finish",
    )(acc)


def solution(mesh):
    in_specs = (
        P("rows", "feat"),
        P("rows", None),
        P("rows"),
        P("rows"),
        P("rows"),
        P(),
        P(),
        P(),
        P(),
    )
    out_specs = (P("rows", None, "feat", None),) * 3
    body = functools.partial(on_device, mesh.shape["rows"], mesh.shape["feat"])
    return jax.shard_map(body, mesh=mesh, in_specs=in_specs, out_specs=out_specs, check_vma=False)
```

```python
import functools

import jax
import jax.numpy as jnp
from jax import lax
from jax.experimental import pallas as pl
from jax.experimental.pallas import tpu as pltpu
from jax.sharding import PartitionSpec as P

BINS = 256
MESH = pl.DeviceIdType.MESH
NT = (((1,), (1,)), ((), ()))
EXTRA = 16
CHUNKS = 4
GROUP = 16
LANES = 128


def partner_of(me, step, owners):
    total, bit = 0, 1
    while bit < owners:
        total = total + lax.rem(me // bit + step // bit, 2) * bit
        bit *= 2
    return total


def fold(extra):
    parts = extra.shape[1] // LANES
    pieces = [extra[0:4, k * LANES : (k + 1) * LANES] for k in range(parts)]
    if parts < 4:
        pieces.append(jnp.zeros((EXTRA - 4 * parts, LANES), extra.dtype))
    return jnp.concatenate(pieces, axis=0)


def unfold(folded, capacity):
    folded = folded.astype(jnp.float32)
    parts = [folded[4 * k : 4 * k + 4] for k in range(capacity // LANES)]
    return jnp.concatenate(parts, axis=1)


def weight_rows(extra):
    slots = extra.shape[1]
    row = lax.broadcasted_iota(jnp.int32, (16, slots), 0)
    kind = row % 3
    value = jnp.where(kind == 0, extra[0:1], jnp.where(kind == 1, extra[1:2], extra[2:3]))
    same = (row // 3).astype(jnp.float32) == extra[3:4]
    return jnp.where(same, value, 0.0).astype(jnp.bfloat16)


def pair_sums(bins, weights):
    slots = bins.shape[1]
    bf = jnp.bfloat16
    high = jnp.floor(bins * (1.0 / 64.0))
    low = (bins - 64.0 * high).astype(bf)
    high = high.astype(bf)
    level = lax.broadcasted_iota(jnp.int32, (16, slots), 0).astype(jnp.float32).astype(bf)
    one, zero = jnp.ones((), bf), jnp.zeros((), bf)
    lane = lax.broadcasted_iota(jnp.int32, (64, 128), 1)
    pairs = []
    for base in range(0, GROUP, 4):
        left, right = [], []
        for f in range(base, base + 4):
            high_f = jnp.broadcast_to(high[f : f + 1], (16, slots))
            low_f = jnp.broadcast_to(low[f : f + 1], (16, slots))
            for c in range(4):
                left.append(jnp.where(high_f == jnp.asarray(c, bf), weights, zero))
                right.append(jnp.where(low_f == level + jnp.asarray(16 * c, bf), one, zero))
        left = jnp.concatenate(left, axis=0)
        right = jnp.concatenate(right, axis=0)
        sums = lax.dot_general(left, right, NT, preferred_element_type=jnp.float32)
        for i in range(2):
            even = sums[128 * i : 128 * i + 64, 128 * i : 128 * i + 128]
            odd = sums[128 * i + 64 : 128 * i + 128, 128 * i : 128 * i + 128]
            pairs.append(jnp.where(lane < 64, even, odd))
    return pairs


def exchange_kernel(
    owners,
    feat_devs,
    node_count,
    capacity,
    bins_hbm,
    node_hbm,
    weight_hbm,
    treat_hbm,
    result_hbm,
    root_feat_hbm,
    root_cut_hbm,
    child_feat_hbm,
    child_cut_hbm,
    acc_ref,
    bins_in,
    node_in,
    weight_in,
    treat_in,
    result_in,
    root_feat_in,
    root_cut_in,
    child_feat_in,
    child_cut_in,
    pick_send,
    pick_recv,
    blocks,
    extra_blocks,
    got,
    got_extra,
    rows_in,
    slot_ref,
    places,
    weights_ref,
    in_sem,
    pick_send_sem,
    pick_recv_sem,
    send_sem,
    recv_sem,
    extra_send_sem,
    extra_recv_sem,
):
    feat_here, rows_here = bins_in.shape
    me = lax.axis_index("rows")
    mine = lax.axis_index("feat")
    bf = jnp.bfloat16

    pairs = [
        (node_hbm, node_in),
        (bins_hbm, bins_in),
        (root_feat_hbm, root_feat_in),
        (child_feat_hbm, child_feat_in),
        (root_cut_hbm, root_cut_in),
        (child_cut_hbm, child_cut_in),
        (weight_hbm, weight_in),
        (treat_hbm, treat_in),
        (result_hbm, result_in),
    ]
    loads = [pltpu.make_async_copy(a, b, in_sem.at[k]) for k, (a, b) in enumerate(pairs)]
    for load in loads:
        load.start()

    barrier = pltpu.get_barrier_semaphore()
    for step in range(1, owners):
        pl.semaphore_signal(
            barrier,
            inc=1,
            device_id={"rows": partner_of(me, step, owners)},
            device_id_type=MESH,
        )
    for step in range(1, feat_devs):
        pl.semaphore_signal(
            barrier, inc=1, device_id={"feat": lax.rem(mine + step, feat_devs)}, device_id_type=MESH
        )

    for load in loads[:2]:
        load.wait()
    node = node_in[...]
    bins = bins_in[...].astype(jnp.float32).astype(bf)
    rows_in[0:feat_here] = bins
    chosen = lax.broadcasted_iota(jnp.int32, (node_count, rows_here), 0) == node

    chunk = 256
    ones = chosen.astype(jnp.float32)
    up_to = lax.broadcasted_iota(jnp.int32, (chunk, chunk), 0) <= lax.broadcasted_iota(
        jnp.int32, (chunk, chunk), 1
    )
    up_to = up_to.astype(jnp.float32).astype(bf)
    before = jnp.zeros((node_count, 1), jnp.float32)
    ranks = []
    for k in range(rows_here // chunk):
        here = ones[:, k * chunk : (k + 1) * chunk]
        counts = jnp.dot(here.astype(bf), up_to, preferred_element_type=jnp.float32) + before
        ranks.append(jnp.sum(here * counts, axis=0, keepdims=True))
        before = before + jnp.sum(here, axis=1, keepdims=True)
    rank = jnp.concatenate(ranks, axis=1).astype(jnp.int32) - 1
    slot_ref[...] = node * capacity + rank

    half = owners // 2
    per = owners // CHUNKS
    block = min(256, capacity)
    level = lax.broadcasted_iota(jnp.int32, (16, rows_here), 0).astype(jnp.float32).astype(bf)
    one, zero = jnp.ones((), bf), jnp.zeros((), bf)

    def fill(step, where):
        target = slot_ref[...] - partner_of(me, step, owners) * capacity

        @pl.loop(0, capacity // block)
        def _(part):
            inside = target - part * block
            inside = jnp.where((inside >= 0) & (inside < block), inside, -1)
            inside = inside.astype(jnp.float32).astype(bf)
            inside = jnp.broadcast_to(inside, (16, rows_here))
            for k in range(0, block, 16):
                rows = pl.ds(pl.multiple_of(part * block + k, 16), 16)
                places[where, rows] = jnp.where(inside == level + jnp.asarray(k, bf), one, zero)

    def pack(step, where):
        moved = lax.dot_general(rows_in[...], places[where], NT, preferred_element_type=jnp.float32)
        blocks[step] = moved[0:feat_here].astype(bf)
        extra_blocks[step] = fold(moved[feat_here : feat_here + EXTRA]).astype(bf)

    def send(step):
        return pltpu.make_async_remote_copy(
            src_ref=blocks.at[step],
            dst_ref=got.at[step],
            send_sem=send_sem.at[step],
            recv_sem=recv_sem.at[step],
            device_id={"rows": partner_of(me, step, owners)},
            device_id_type=MESH,
        )

    def send_extra(step):
        return pltpu.make_async_remote_copy(
            src_ref=extra_blocks.at[step],
            dst_ref=got_extra.at[step],
            send_sem=extra_send_sem.at[step],
            recv_sem=extra_recv_sem.at[step],
            device_id={"rows": partner_of(me, step, owners)},
            device_id_type=MESH,
        )

    def far(step):
        fill(step, step - half)
        moved = lax.dot_general(
            rows_in[0:feat_here], places[step - half], NT, preferred_element_type=jnp.float32
        )
        blocks[step] = moved.astype(bf)
        send(step).start()

    pl.semaphore_wait(barrier, owners - 1 + feat_devs - 1)
    far(half)

    for load in loads[2:]:
        load.wait()

    def column(table, stride, first):
        width = table.shape[1]
        spot = lax.broadcasted_iota(jnp.int32, (node_count, width), 0) * stride + first
        lane = lax.broadcasted_iota(jnp.int32, (node_count, width), 1)
        picked = jnp.where(lane == spot, table.astype(jnp.float32), 0.0)
        return jnp.sum(picked, axis=1, keepdims=True)

    wanted = [
        column(root_feat_in[...], 1, 0),
        column(child_feat_in[...], 2, 0),
        column(child_feat_in[...], 2, 1),
    ]
    limits = [
        column(root_cut_in[...], 1, 0),
        column(child_cut_in[...], 2, 0),
        column(child_cut_in[...], 2, 1),
    ]
    local = lax.broadcasted_iota(jnp.int32, (node_count, feat_here), 1) + mine * feat_here
    local = local.astype(jnp.float32)
    pick = jnp.concatenate([jnp.where(local == w, 1.0, 0.0) for w in wanted], axis=0).astype(bf)
    table = jnp.dot(pick, bins, preferred_element_type=jnp.float32)
    picks, cuts = [], []
    for kind in range(3):
        part = table[kind * node_count : (kind + 1) * node_count]
        picks.append(jnp.sum(jnp.where(chosen, part, 0.0), axis=0, keepdims=True))
        limit = jnp.broadcast_to(limits[kind], (node_count, rows_here))
        cuts.append(jnp.sum(jnp.where(chosen, limit, 0.0), axis=0, keepdims=True))
    picks.append(jnp.zeros_like(picks[0]))
    picks = jnp.concatenate(picks, axis=0)
    quarter = rows_here // 4
    folded = jnp.concatenate([picks[:, k * quarter : (k + 1) * quarter] for k in range(4)], axis=0)
    pick_send[...] = folded.astype(bf)

    pick_copies = []
    for step in range(1, feat_devs):
        copy = pltpu.make_async_remote_copy(
            src_ref=pick_send,
            dst_ref=pick_recv.at[step - 1],
            send_sem=pick_send_sem.at[step - 1],
            recv_sem=pick_recv_sem.at[step - 1],
            device_id={"feat": lax.rem(mine + step, feat_devs)},
            device_id_type=MESH,
        )
        copy.start()
        pick_copies.append(copy)

    @pl.loop(half + 1, owners)
    def _(step):
        far(step)

    weight, treat, result = weight_in[...], treat_in[...], result_in[...]
    scaled = weight * treat
    for copy in pick_copies:
        copy.wait()
    total = folded
    for step in range(feat_devs - 1):
        total = total + pick_recv[step].astype(jnp.float32)
    split = jnp.concatenate([total[4 * k : 4 * k + 4] for k in range(4)], axis=1)
    right_root = split[0:1] > cuts[0]
    first = jnp.where(split[1:2] > cuts[1], 1.0, 0.0)
    second = jnp.where(split[2:3] > cuts[2], 1.0, 0.0)
    leaf = jnp.where(right_root, 2.0 + second, first)
    none = jnp.zeros((EXTRA - 4, rows_here), jnp.float32)
    extra = jnp.concatenate([weight, scaled * treat, scaled * result, leaf, none], axis=0)
    rows_in[feat_here : feat_here + EXTRA] = extra.astype(bf)

    @pl.loop(half, owners)
    def _(step):
        moved = lax.dot_general(
            rows_in[feat_here : feat_here + EXTRA],
            places[step - half],
            NT,
            preferred_element_type=jnp.float32,
        )
        extra_blocks[step] = fold(moved).astype(bf)
        send_extra(step).start()

    @pl.loop(0, half)
    def _(back):
        step = half - 1 - back
        fill(step, step)
        pack(step, step)

        @pl.when(step > 0)
        def _():
            send(step).start()
            send_extra(step).start()

    got[0] = blocks[0]
    got_extra[0] = extra_blocks[0]
    acc_ref[...] = jnp.zeros_like(acc_ref)

    @pl.loop(0, CHUNKS)
    def _(c):
        for s in range(per):
            step = c * per + s

            @pl.when(step > 0)
            def _():
                send(step).wait_recv()
                send_extra(step).wait_recv()

        known = [unfold(got_extra[c * per + s], capacity) for s in range(per)]
        weights_ref[...] = weight_rows(jnp.concatenate(known, axis=1))

        @pl.loop(0, feat_here // GROUP)
        def _(part):
            rows = pl.ds(pl.multiple_of(part * GROUP, GROUP), GROUP)
            values = jnp.concatenate([got[c * per + s, rows] for s in range(per)], axis=1)
            for k, sums in enumerate(pair_sums(values.astype(jnp.float32), weights_ref[...])):
                acc_ref[part * (GROUP // 2) + k] += sums

    @pl.loop(1, owners)
    def _(step):
        send(step).wait_send()
        send_extra(step).wait_send()


def finish_kernel(acc_ref, node_out, child_out, leaf_out, whole):
    lane = lax.broadcasted_iota(jnp.int32, (16, 128), 1)
    group = 2 * acc_ref.shape[0]
    for k in range(group // 2):
        part = acc_ref[k]
        parts = [part[16 * c : 16 * c + 16] for c in range(4)]
        turned = [pltpu.roll(p, 64, 1) for p in parts]
        for i in range(2):
            f = 2 * k + i
            for t in range(2):
                if i == 0:
                    full = jnp.where(lane < 64, parts[2 * t], turned[2 * t + 1])
                else:
                    full = jnp.where(lane < 64, turned[2 * t], parts[2 * t + 1])
                whole[t, 16 * f : 16 * f + 16] = full
    for t in range(2):
        lanes = slice(128 * t, 128 * t + 128)
        for m in range(3):
            leaves = []
            for q in range(4):
                leaf = whole[t, pl.ds(3 * q + m, group, stride=16)]
                leaf_out[q, m, :, lanes] = leaf
                leaves.append(leaf)
            left, right = leaves[0] + leaves[1], leaves[2] + leaves[3]
            child_out[0, m, :, lanes] = left
            child_out[1, m, :, lanes] = right
            node_out[0, m, :, lanes] = left + right


def on_device(
    owners,
    feat_devs,
    binned,
    node_index,
    treatment,
    outcome,
    unit_weight,
    root_feature,
    root_cutoff,
    child_feature,
    child_cutoff,
):
    rows_here, feat_here = binned.shape
    node_count = root_feature.shape[0]
    assert node_count == owners and owners >= 2 * CHUNKS and owners & (owners - 1) == 0
    capacity = 2 * rows_here // node_count
    bf, f32, i32 = jnp.bfloat16, jnp.float32, jnp.int32
    per = owners // CHUNKS
    dma = pltpu.SemaphoreType.DMA
    anywhere = pl.BlockSpec(memory_space=pltpu.HBM)
    vmem = pl.BlockSpec(memory_space=pltpu.VMEM)
    acc = pl.pallas_call(
        functools.partial(exchange_kernel, owners, feat_devs, node_count, capacity),
        out_shape=jax.ShapeDtypeStruct((feat_here // 2, 64, 128), f32),
        in_specs=[anywhere] * 9,
        out_specs=vmem,
        scratch_shapes=[
            pltpu.VMEM((feat_here, rows_here), i32),
            pltpu.VMEM((1, rows_here), i32),
            pltpu.VMEM((1, rows_here), f32),
            pltpu.VMEM((1, rows_here), f32),
            pltpu.VMEM((1, rows_here), f32),
            pltpu.VMEM((1, node_count), i32),
            pltpu.VMEM((1, node_count), i32),
            pltpu.VMEM((1, 2 * node_count), i32),
            pltpu.VMEM((1, 2 * node_count), i32),
            pltpu.VMEM((16, rows_here // 4), bf),
            pltpu.VMEM((feat_devs - 1, 16, rows_here // 4), bf),
            pltpu.VMEM((owners, feat_here, capacity), bf),
            pltpu.VMEM((owners, EXTRA, LANES), bf),
            pltpu.VMEM((owners, feat_here, capacity), bf),
            pltpu.VMEM((owners, EXTRA, LANES), bf),
            pltpu.VMEM((feat_here + EXTRA, rows_here), bf),
            pltpu.VMEM((1, rows_here), i32),
            pltpu.VMEM((owners // 2, capacity, rows_here), bf),
            pltpu.VMEM((16, per * capacity), bf),
            dma((9,)),
            dma((feat_devs - 1,)),
            dma((feat_devs - 1,)),
            dma((owners,)),
            dma((owners,)),
            dma((owners,)),
            dma((owners,)),
        ],
        compiler_params=pltpu.CompilerParams(
            collective_id=0, has_side_effects=True, vmem_limit_bytes=64 * 1024 * 1024
        ),
        name="exchange",
    )(
        binned.T,
        node_index.reshape(1, rows_here),
        unit_weight.reshape(1, rows_here),
        treatment.reshape(1, rows_here),
        outcome.reshape(1, rows_here),
        root_feature.reshape(1, node_count),
        root_cutoff.reshape(1, node_count),
        child_feature.reshape(1, 2 * node_count),
        child_cutoff.reshape(1, 2 * node_count),
    )

    return pl.pallas_call(
        finish_kernel,
        grid=(feat_here // GROUP,),
        out_shape=tuple(
            jax.ShapeDtypeStruct((k, 3, feat_here, BINS), f32) for k in (1, 2, 4)
        ),
        in_specs=[
            pl.BlockSpec((GROUP // 2, 64, 128), lambda i: (i, 0, 0)),
        ],
        out_specs=tuple(pl.BlockSpec((k, 3, GROUP, BINS), lambda i: (0, 0, i, 0)) for k in (1, 2, 4)),
        scratch_shapes=[pltpu.VMEM((2, GROUP * 16, 128), f32)],
        compiler_params=pltpu.CompilerParams(vmem_limit_bytes=64 * 1024 * 1024),
        name="finish",
    )(acc)


def solution(mesh):
    in_specs = (
        P("rows", "feat"),
        P("rows", None),
        P("rows"),
        P("rows"),
        P("rows"),
        P(),
        P(),
        P(),
        P(),
    )
    out_specs = (P("rows", None, "feat", None),) * 3
    body = functools.partial(on_device, mesh.shape["rows"], mesh.shape["feat"])
    return jax.shard_map(body, mesh=mesh, in_specs=in_specs, out_specs=out_specs, check_vma=False)
```

```python
import functools

import jax
import jax.numpy as jnp
from jax import lax
from jax.experimental import pallas as pl
from jax.experimental.pallas import tpu as pltpu
from jax.sharding import PartitionSpec as P

BINS = 256
MESH = pl.DeviceIdType.MESH
NT = (((1,), (1,)), ((), ()))
EXTRA = 16
CHUNKS = 4
GROUP = 16
LANES = 128


def partner_of(me, step, owners):
    total, bit = 0, 1
    while bit < owners:
        total = total + lax.rem(me // bit + step // bit, 2) * bit
        bit *= 2
    return total


def fold(extra):
    parts = extra.shape[1] // LANES
    pieces = [extra[0:4, k * LANES : (k + 1) * LANES] for k in range(parts)]
    if parts < 4:
        pieces.append(jnp.zeros((EXTRA - 4 * parts, LANES), extra.dtype))
    return jnp.concatenate(pieces, axis=0)


def unfold(folded, capacity):
    folded = folded.astype(jnp.float32)
    parts = [folded[4 * k : 4 * k + 4] for k in range(capacity // LANES)]
    return jnp.concatenate(parts, axis=1)


def weight_rows(extra):
    slots = extra.shape[1]
    row = lax.broadcasted_iota(jnp.int32, (16, slots), 0)
    kind = row % 3
    value = jnp.where(kind == 0, extra[0:1], jnp.where(kind == 1, extra[1:2], extra[2:3]))
    same = (row // 3).astype(jnp.float32) == extra[3:4]
    return jnp.where(same, value, 0.0).astype(jnp.bfloat16)


def pair_sums(bins, weights):
    slots = bins.shape[1]
    bf = jnp.bfloat16
    high = jnp.floor(bins * (1.0 / 64.0))
    low = (bins - 64.0 * high).astype(bf)
    high = high.astype(bf)
    level = lax.broadcasted_iota(jnp.int32, (16, slots), 0).astype(jnp.float32).astype(bf)
    one, zero = jnp.ones((), bf), jnp.zeros((), bf)
    lane = lax.broadcasted_iota(jnp.int32, (64, 128), 1)
    pairs = []
    for base in range(0, GROUP, 4):
        left, right = [], []
        for f in range(base, base + 4):
            high_f = jnp.broadcast_to(high[f : f + 1], (16, slots))
            low_f = jnp.broadcast_to(low[f : f + 1], (16, slots))
            for c in range(4):
                left.append(jnp.where(high_f == jnp.asarray(c, bf), weights, zero))
                right.append(jnp.where(low_f == level + jnp.asarray(16 * c, bf), one, zero))
        left = jnp.concatenate(left, axis=0)
        right = jnp.concatenate(right, axis=0)
        sums = lax.dot_general(left, right, NT, preferred_element_type=jnp.float32)
        for i in range(2):
            even = sums[128 * i : 128 * i + 64, 128 * i : 128 * i + 128]
            odd = sums[128 * i + 64 : 128 * i + 128, 128 * i : 128 * i + 128]
            pairs.append(jnp.where(lane < 64, even, odd))
    return pairs


def exchange_kernel(
    owners,
    feat_devs,
    node_count,
    capacity,
    bins_hbm,
    node_hbm,
    weight_hbm,
    treat_hbm,
    result_hbm,
    root_feat_hbm,
    root_cut_hbm,
    child_feat_hbm,
    child_cut_hbm,
    late_ref,
    late_extra_ref,
    acc_ref,
    bins_in,
    node_in,
    weight_in,
    treat_in,
    result_in,
    root_feat_in,
    root_cut_in,
    child_feat_in,
    child_cut_in,
    pick_send,
    pick_recv,
    blocks,
    extra_blocks,
    got,
    got_extra,
    rows_in,
    slot_ref,
    places,
    weights_ref,
    in_sem,
    pick_send_sem,
    pick_recv_sem,
    send_sem,
    recv_sem,
    extra_send_sem,
    extra_recv_sem,
):
    feat_here, rows_here = bins_in.shape
    me = lax.axis_index("rows")
    mine = lax.axis_index("feat")
    bf = jnp.bfloat16

    pairs = [
        (node_hbm, node_in),
        (bins_hbm, bins_in),
        (root_feat_hbm, root_feat_in),
        (child_feat_hbm, child_feat_in),
        (root_cut_hbm, root_cut_in),
        (child_cut_hbm, child_cut_in),
        (weight_hbm, weight_in),
        (treat_hbm, treat_in),
        (result_hbm, result_in),
    ]
    loads = [pltpu.make_async_copy(a, b, in_sem.at[k]) for k, (a, b) in enumerate(pairs)]
    for load in loads:
        load.start()

    barrier = pltpu.get_barrier_semaphore()
    for step in range(1, owners):
        pl.semaphore_signal(
            barrier,
            inc=1,
            device_id={"rows": partner_of(me, step, owners)},
            device_id_type=MESH,
        )
    for step in range(1, feat_devs):
        pl.semaphore_signal(
            barrier, inc=1, device_id={"feat": lax.rem(mine + step, feat_devs)}, device_id_type=MESH
        )

    for load in loads:
        load.wait()
    node = node_in[...]
    bins = bins_in[...].astype(jnp.float32).astype(bf)
    rows_in[0:feat_here] = bins
    chosen = lax.broadcasted_iota(jnp.int32, (node_count, rows_here), 0) == node

    def column(table, stride, first):
        width = table.shape[1]
        spot = lax.broadcasted_iota(jnp.int32, (node_count, width), 0) * stride + first
        lane = lax.broadcasted_iota(jnp.int32, (node_count, width), 1)
        picked = jnp.where(lane == spot, table.astype(jnp.float32), 0.0)
        return jnp.sum(picked, axis=1, keepdims=True)

    wanted = [
        column(root_feat_in[...], 1, 0),
        column(child_feat_in[...], 2, 0),
        column(child_feat_in[...], 2, 1),
    ]
    limits = [
        column(root_cut_in[...], 1, 0),
        column(child_cut_in[...], 2, 0),
        column(child_cut_in[...], 2, 1),
    ]
    local = lax.broadcasted_iota(jnp.int32, (node_count, feat_here), 1) + mine * feat_here
    local = local.astype(jnp.float32)
    pick = jnp.concatenate([jnp.where(local == w, 1.0, 0.0) for w in wanted], axis=0).astype(bf)
    table = jnp.dot(pick, bins, preferred_element_type=jnp.float32)
    picks, cuts = [], []
    for kind in range(3):
        part = table[kind * node_count : (kind + 1) * node_count]
        picks.append(jnp.sum(jnp.where(chosen, part, 0.0), axis=0, keepdims=True))
        limit = jnp.broadcast_to(limits[kind], (node_count, rows_here))
        cuts.append(jnp.sum(jnp.where(chosen, limit, 0.0), axis=0, keepdims=True))
    picks.append(jnp.zeros_like(picks[0]))
    picks = jnp.concatenate(picks, axis=0)
    quarter = rows_here // 4
    folded = jnp.concatenate([picks[:, k * quarter : (k + 1) * quarter] for k in range(4)], axis=0)
    pick_send[...] = folded.astype(bf)

    pl.semaphore_wait(barrier, owners - 1 + feat_devs - 1)

    pick_copies = []
    for step in range(1, feat_devs):
        copy = pltpu.make_async_remote_copy(
            src_ref=pick_send,
            dst_ref=pick_recv.at[step - 1],
            send_sem=pick_send_sem.at[step - 1],
            recv_sem=pick_recv_sem.at[step - 1],
            device_id={"feat": lax.rem(mine + step, feat_devs)},
            device_id_type=MESH,
        )
        copy.start()
        pick_copies.append(copy)

    chunk = 256
    ones = chosen.astype(jnp.float32)
    up_to = lax.broadcasted_iota(jnp.int32, (chunk, chunk), 0) <= lax.broadcasted_iota(
        jnp.int32, (chunk, chunk), 1
    )
    up_to = up_to.astype(jnp.float32).astype(bf)
    before = jnp.zeros((node_count, 1), jnp.float32)
    ranks = []
    for k in range(rows_here // chunk):
        here = ones[:, k * chunk : (k + 1) * chunk]
        counts = jnp.dot(here.astype(bf), up_to, preferred_element_type=jnp.float32) + before
        ranks.append(jnp.sum(here * counts, axis=0, keepdims=True))
        before = before + jnp.sum(here, axis=1, keepdims=True)
    rank = jnp.concatenate(ranks, axis=1).astype(jnp.int32) - 1
    slot_ref[...] = node * capacity + rank

    half = owners // 2
    per = owners // CHUNKS
    late_first = owners - per
    block = min(256, capacity)
    level = lax.broadcasted_iota(jnp.int32, (16, rows_here), 0).astype(jnp.float32).astype(bf)
    one, zero = jnp.ones((), bf), jnp.zeros((), bf)

    def fill(step, where):
        target = slot_ref[...] - partner_of(me, step, owners) * capacity
        for start in range(0, capacity, block):
            inside = target - start
            inside = jnp.where((inside >= 0) & (inside < block), inside, -1)
            inside = inside.astype(jnp.float32).astype(bf)
            inside = jnp.broadcast_to(inside, (16, rows_here))
            for k in range(0, block, 16):
                places[where, start + k : start + k + 16] = jnp.where(
                    inside == level + jnp.asarray(k, bf), one, zero
                )

    def moved(first, last, where):
        return lax.dot_general(
            rows_in[first:last], places[where], NT, preferred_element_type=jnp.float32
        )

    def send(step, late):
        return pltpu.make_async_remote_copy(
            src_ref=blocks.at[step],
            dst_ref=late_ref.at[step - late_first] if late else got.at[step],
            send_sem=send_sem.at[step],
            recv_sem=recv_sem.at[step],
            device_id={"rows": partner_of(me, step, owners)},
            device_id_type=MESH,
        )

    def send_extra(step, late):
        return pltpu.make_async_remote_copy(
            src_ref=extra_blocks.at[step],
            dst_ref=late_extra_ref.at[step - late_first] if late else got_extra.at[step],
            send_sem=extra_send_sem.at[step],
            recv_sem=extra_recv_sem.at[step],
            device_id={"rows": partner_of(me, step, owners)},
            device_id_type=MESH,
        )

    for start, stop, late in ((half, late_first, False), (late_first, owners, True)):

        @pl.loop(start, stop)
        def _(step):
            fill(step, step - half)
            blocks[step] = moved(0, feat_here, step - half).astype(bf)
            send(step, late).start()

    weight, treat, result = weight_in[...], treat_in[...], result_in[...]
    scaled = weight * treat
    for copy in pick_copies:
        copy.wait()
    total = folded
    for step in range(feat_devs - 1):
        total = total + pick_recv[step].astype(jnp.float32)
    split = jnp.concatenate([total[4 * k : 4 * k + 4] for k in range(4)], axis=1)
    right_root = split[0:1] > cuts[0]
    first = jnp.where(split[1:2] > cuts[1], 1.0, 0.0)
    second = jnp.where(split[2:3] > cuts[2], 1.0, 0.0)
    leaf = jnp.where(right_root, 2.0 + second, first)
    none = jnp.zeros((EXTRA - 4, rows_here), jnp.float32)
    extra = jnp.concatenate([weight, scaled * treat, scaled * result, leaf, none], axis=0)
    rows_in[feat_here : feat_here + EXTRA] = extra.astype(bf)

    for start, stop, late in ((half, late_first, False), (late_first, owners, True)):

        @pl.loop(start, stop)
        def _(step):
            tail = moved(feat_here, feat_here + EXTRA, step - half)
            extra_blocks[step] = fold(tail).astype(bf)
            send_extra(step, late).start()

    @pl.loop(1, half)
    def _(back):
        step = half - back
        fill(step, step)
        both = moved(0, feat_here + EXTRA, step)
        blocks[step] = both[0:feat_here].astype(bf)
        extra_blocks[step] = fold(both[feat_here : feat_here + EXTRA]).astype(bf)
        send(step, False).start()
        send_extra(step, False).start()

    fill(0, 0)
    both = moved(0, feat_here + EXTRA, 0)
    got[0] = both[0:feat_here].astype(bf)
    got_extra[0] = fold(both[feat_here : feat_here + EXTRA]).astype(bf)

    for c in range(CHUNKS - 1):
        for step in range(max(1, c * per), (c + 1) * per):
            send(step, False).wait_recv()
            send_extra(step, False).wait_recv()
        known = [unfold(got_extra[c * per + s], capacity) for s in range(per)]
        known = jnp.concatenate(known, axis=1)
        weights_ref[...] = weight_rows(known)

        @pl.loop(0, feat_here // GROUP)
        def _(block):
            rows = pl.ds(pl.multiple_of(block * GROUP, GROUP), GROUP)
            values = jnp.concatenate([got[c * per + s, rows] for s in range(per)], axis=1)
            sums = pair_sums(values.astype(jnp.float32), weights_ref[...])
            for k, part in enumerate(sums):
                spot = block * (GROUP // 2) + k
                acc_ref[spot] = part if c == 0 else acc_ref[spot] + part

    for step in range(1, owners):
        send(step, step >= late_first).wait_send()
        send_extra(step, step >= late_first).wait_send()
    for step in range(late_first, owners):
        send(step, True).wait_recv()
        send_extra(step, True).wait_recv()


def finish_kernel(late_ref, extra_ref, acc_ref, node_out, child_out, leaf_out, whole):
    sources, group, capacity = late_ref.shape
    extra = [unfold(extra_ref[s], capacity) for s in range(sources)]
    extra = jnp.concatenate(extra, axis=1)
    bins = jnp.concatenate([late_ref[s] for s in range(sources)], axis=1).astype(jnp.float32)
    lane = lax.broadcasted_iota(jnp.int32, (16, 128), 1)
    for k, part in enumerate(pair_sums(bins, weight_rows(extra))):
        part = part + acc_ref[k]
        parts = [part[16 * c : 16 * c + 16] for c in range(4)]
        turned = [pltpu.roll(p, 64, 1) for p in parts]
        for i in range(2):
            f = 2 * k + i
            for t in range(2):
                if i == 0:
                    full = jnp.where(lane < 64, parts[2 * t], turned[2 * t + 1])
                else:
                    full = jnp.where(lane < 64, turned[2 * t], parts[2 * t + 1])
                whole[t, 16 * f : 16 * f + 16] = full
    for t in range(2):
        lanes = slice(128 * t, 128 * t + 128)
        for m in range(3):
            leaves = []
            for q in range(4):
                leaf = whole[t, pl.ds(3 * q + m, group, stride=16)]
                leaf_out[q, m, :, lanes] = leaf
                leaves.append(leaf)
            left, right = leaves[0] + leaves[1], leaves[2] + leaves[3]
            child_out[0, m, :, lanes] = left
            child_out[1, m, :, lanes] = right
            node_out[0, m, :, lanes] = left + right


def on_device(
    owners,
    feat_devs,
    binned,
    node_index,
    treatment,
    outcome,
    unit_weight,
    root_feature,
    root_cutoff,
    child_feature,
    child_cutoff,
):
    rows_here, feat_here = binned.shape
    node_count = root_feature.shape[0]
    assert node_count == owners and owners >= 2 * CHUNKS and owners & (owners - 1) == 0
    capacity = 2 * rows_here // node_count
    bf, f32, i32 = jnp.bfloat16, jnp.float32, jnp.int32
    per = owners // CHUNKS
    dma = pltpu.SemaphoreType.DMA
    anywhere = pl.BlockSpec(memory_space=pltpu.HBM)
    vmem = pl.BlockSpec(memory_space=pltpu.VMEM)
    late, late_extra, acc = pl.pallas_call(
        functools.partial(exchange_kernel, owners, feat_devs, node_count, capacity),
        out_shape=(
            jax.ShapeDtypeStruct((per, feat_here, capacity), bf),
            jax.ShapeDtypeStruct((per, EXTRA, LANES), bf),
            jax.ShapeDtypeStruct((feat_here // 2, 64, 128), f32),
        ),
        in_specs=[anywhere] * 9,
        out_specs=(anywhere, anywhere, vmem),
        scratch_shapes=[
            pltpu.VMEM((feat_here, rows_here), i32),
            pltpu.VMEM((1, rows_here), i32),
            pltpu.VMEM((1, rows_here), f32),
            pltpu.VMEM((1, rows_here), f32),
            pltpu.VMEM((1, rows_here), f32),
            pltpu.VMEM((1, node_count), i32),
            pltpu.VMEM((1, node_count), i32),
            pltpu.VMEM((1, 2 * node_count), i32),
            pltpu.VMEM((1, 2 * node_count), i32),
            pltpu.VMEM((16, rows_here // 4), bf),
            pltpu.VMEM((feat_devs - 1, 16, rows_here // 4), bf),
            pltpu.VMEM((owners, feat_here, capacity), bf),
            pltpu.VMEM((owners, EXTRA, LANES), bf),
            pltpu.VMEM((owners - per, feat_here, capacity), bf),
            pltpu.VMEM((owners - per, EXTRA, LANES), bf),
            pltpu.VMEM((feat_here + EXTRA, rows_here), bf),
            pltpu.VMEM((1, rows_here), i32),
            pltpu.VMEM((owners // 2, capacity, rows_here), bf),
            pltpu.VMEM((16, per * capacity), bf),
            dma((9,)),
            dma((feat_devs - 1,)),
            dma((feat_devs - 1,)),
            dma((owners,)),
            dma((owners,)),
            dma((owners,)),
            dma((owners,)),
        ],
        compiler_params=pltpu.CompilerParams(
            collective_id=0, has_side_effects=True, vmem_limit_bytes=64 * 1024 * 1024
        ),
        name="exchange",
    )(
        binned.T,
        node_index.reshape(1, rows_here),
        unit_weight.reshape(1, rows_here),
        treatment.reshape(1, rows_here),
        outcome.reshape(1, rows_here),
        root_feature.reshape(1, node_count),
        root_cutoff.reshape(1, node_count),
        child_feature.reshape(1, 2 * node_count),
        child_cutoff.reshape(1, 2 * node_count),
    )

    return pl.pallas_call(
        finish_kernel,
        grid=(feat_here // GROUP,),
        out_shape=tuple(
            jax.ShapeDtypeStruct((k, 3, feat_here, BINS), f32) for k in (1, 2, 4)
        ),
        in_specs=[
            pl.BlockSpec((per, GROUP, capacity), lambda i: (0, i, 0)),
            pl.BlockSpec((per, EXTRA, LANES), lambda i: (0, 0, 0)),
            pl.BlockSpec((GROUP // 2, 64, 128), lambda i: (i, 0, 0)),
        ],
        out_specs=tuple(pl.BlockSpec((k, 3, GROUP, BINS), lambda i: (0, 0, i, 0)) for k in (1, 2, 4)),
        scratch_shapes=[pltpu.VMEM((2, GROUP * 16, 128), f32)],
        compiler_params=pltpu.CompilerParams(vmem_limit_bytes=64 * 1024 * 1024),
        name="finish",
    )(late, late_extra, acc)


def solution(mesh):
    in_specs = (
        P("rows", "feat"),
        P("rows", None),
        P("rows"),
        P("rows"),
        P("rows"),
        P(),
        P(),
        P(),
        P(),
    )
    out_specs = (P("rows", None, "feat", None),) * 3
    body = functools.partial(on_device, mesh.shape["rows"], mesh.shape["feat"])
    return jax.shard_map(body, mesh=mesh, in_specs=in_specs, out_specs=out_specs, check_vma=False)
```
